128 devices in a mesh: rows: 128 (over y, x, z, core).
Axes of the slice: x: 4, y: 4, z: 4, core: 2. Of those that a mesh axis runs over, the one named last changes fastest.
Arguments:
- vectors: float32 [262144, 128], P('rows'), may hold values from -6.05 to 6.05
- hblocks: float32 [2048, 20, 128, 128], P('rows'), may hold values from -1 to 1
- local_cols: int32 [2048, 20], P('rows'), may hold values from 0 to 47, as said below
- ghost_lists: int32 [128, 4, 8], replicated, may hold values from 0 to 15, as said below
Outputs:
- basis: float32 [262144, 128], P('rows')
- factor: float32 [128, 128], replicated
The draws below stay inside these ranges and needn't reach their ends.
Inputs may be any that keep to these rules, and one draw needn't show every extreme that they name: `ghost_lists`: each list names 8 different blocks of the sending device. `local_cols`: each block row names 20 different slots.
All inputs are finite; a program needn't handle non-finite values.
Results may differ from the reference program's by a relative error of at most 0.0003.
Values sent between devices are 32-bit elements; how exact they have to be, the bound alone decides.
No kernel may reach another device: no remote copies, remote signals or barrier semaphores. Data moves between devices by JAX's collectives and lax.ppermute only.
A program may use at most 128 MiB of HBM per device.

```python
import jax
import jax.numpy as jnp
from jax import lax

BS = 128
W = 128
RB = 16
REACH = 2
GHOST = 8
NNZB = 20
NBR = 2048
N = 262144
DEVICES = 128


def draw_ghost_lists(key, part):
    key = jax.random.fold_in(key, 1)
    keys = jax.random.split(key, DEVICES * 2 * REACH)
    lists = jax.vmap(lambda k: jax.random.permutation(k, RB)[:GHOST])(keys)
    return lists.reshape(DEVICES, 2 * REACH, GHOST).astype(jnp.int32)


def draw_local_cols(key, part):
    key = jax.random.fold_in(key, 2)
    keys = jax.random.split(key, NBR)
    pool = RB + 2 * REACH * GHOST
    cols = jax.vmap(lambda k: jax.random.permutation(k, pool)[:NNZB])(keys)
    return cols.astype(jnp.int32)


def draw_vectors(key, part):
    key = jax.random.fold_in(key, 3)
    key_common, key_scale, key_sign, key_noise, key_weight, key_wsign = jax.random.split(key, 6)
    common = jnp.clip(jax.random.normal(key_common, (N, 2), jnp.float32), -1.5, 1.5)
    noise = jnp.clip(jax.random.normal(key_noise, (N, W), jnp.float32), -5.0, 5.0)
    scales = jax.random.uniform(key_scale, (1, W), jnp.float32, 0.5, 1.5)
    signs = jnp.where(jax.random.bernoulli(key_sign, 0.5, (1, W)), 1.0, -1.0).astype(jnp.float32)
    weights = jax.random.uniform(key_weight, (2, W), jnp.float32, 0.5, 1.0)
    wsigns = jnp.where(jax.random.bernoulli(key_wsign, 0.5, (2, W)), 1.0, -1.0).astype(jnp.float32)
    weights = weights * wsigns
    flat = jnp.ones((N, 1), jnp.float32) * (scales * signs)
    spread = common[:, 0:1] * weights[0:1, :] + common[:, 1:2] * weights[1:2, :]
    return (flat + spread + 0.02 * noise).astype(jnp.float32)


def draw_hblocks(key, part):
    key = jax.random.fold_in(key, 4)
    sigma = float(NNZB * BS) ** (-0.5)
    raw = jnp.clip(jax.random.normal(key, (NBR, NNZB, BS, BS), jnp.float32), -4.0, 4.0)
    raw = raw * sigma
    centred = raw - jnp.mean(raw, axis=(1, 3), keepdims=True)
    return (centred + 1.2071067811865475 / float(NNZB * BS)).astype(jnp.float32)


def setup_inputs(seed: int = 0) -> dict:
    arg_keys = jax.random.split(jax.random.key(seed), 5)
    return {
        "vectors": draw_vectors(jax.random.fold_in(arg_keys[4], 71), 0),
        "hblocks": draw_hblocks(jax.random.fold_in(arg_keys[4], 71), 0),
        "local_cols": draw_local_cols(jax.random.fold_in(arg_keys[4], 71), 0),
        "ghost_lists": draw_ghost_lists(jax.random.fold_in(arg_keys[4], 71), 0),
    }


def offsets_list():
    return [o for o in range(-REACH, REACH + 1) if o != 0]

def column_blocks(local_cols, ghost_lists):
    devs = jnp.arange(DEVICES, dtype=jnp.int32)
    parts = [devs[:, None] * RB + jnp.arange(RB, dtype=jnp.int32)[None, :]]
    for k, off in enumerate(offsets_list()):
        source = (devs + off) % DEVICES
        parts.append(source[:, None] * RB + ghost_lists[source, k])
    table = jnp.concatenate(parts, axis=1)
    owner = (jnp.arange(NBR, dtype=jnp.int32) // RB).astype(jnp.int32)
    return table[owner[:, None], local_cols]

def apply_ham(hblocks, cols, vectors):
    blocks = vectors.reshape(NBR, BS, W)

    def one_row(item):
        hrow, crow = item
        picked = blocks[crow]
        return jnp.einsum('nij,njk->ik', hrow, picked, precision=lax.Precision.HIGHEST)
    return lax.map(one_row, (hblocks, cols)).reshape(N, W)

def lower_cholesky(gram):
    size = gram.shape[0]
    index_all = jnp.arange(size, dtype=jnp.int32)

    def column_step(j, lower):
        row_j = lax.dynamic_index_in_dim(lower, j, 0, keepdims=False)
        col_a = lax.dynamic_index_in_dim(gram, j, 1, keepdims=False)
        rest = col_a - jnp.dot(lower, row_j, precision=lax.Precision.HIGHEST)
        pivot = jnp.sqrt(lax.dynamic_index_in_dim(rest, j, 0, keepdims=False))
        column = jnp.where(index_all > j, rest / pivot, jnp.where(index_all == j, pivot, 0.0))
        return lower + column[:, None] * (index_all[None, :] == j).astype(gram.dtype)
    return lax.fori_loop(0, size, column_step, jnp.zeros_like(gram))

def upper_inverse(upper):
    size = upper.shape[0]
    eye = jnp.eye(size, dtype=upper.dtype)

    def row_step(t, inverse):
        i = size - 1 - t
        row_u = lax.dynamic_index_in_dim(upper, i, 0, keepdims=False)
        diag = lax.dynamic_index_in_dim(row_u, i, 0, keepdims=False)
        row_e = lax.dynamic_index_in_dim(eye, i, 0, keepdims=False)
        new_row = (row_e - jnp.dot(row_u, inverse, precision=lax.Precision.HIGHEST)) / diag
        return lax.dynamic_update_index_in_dim(inverse, new_row, i, 0)
    return lax.fori_loop(0, size, row_step, jnp.zeros_like(upper))

def upper_factor(mat):
    gram = jnp.dot(mat.T, mat, precision=lax.Precision.HIGHEST) / N
    return lower_cholesky(gram).T

def reference(vectors, hblocks, local_cols, ghost_lists):
    cols = column_blocks(local_cols, ghost_lists)
    first = apply_ham(hblocks, cols, vectors) - 0.5 * vectors
    second = 2.0 * (apply_ham(hblocks, cols, first) - 0.5 * first) - vectors
    upper_one = upper_factor(second)
    middle = jnp.dot(second, upper_inverse(upper_one), precision=lax.Precision.HIGHEST)
    upper_two = upper_factor(middle)
    basis = jnp.dot(middle, upper_inverse(upper_two), precision=lax.Precision.HIGHEST)
    factor = jnp.dot(upper_two, upper_one, precision=lax.Precision.HIGHEST)
    return (basis, factor)
```

```python
import functools

import jax
import jax.numpy as jnp
from jax import lax
from jax.experimental import pallas as pl
from jax.experimental.pallas import tpu as pltpu
from jax.sharding import PartitionSpec as P

BS = 128
W = 128
RB = 16
GHOST = 8
NNZB = 20
NE = RB * NNZB
SPLIT = 3
VZERO = 48
MAXE = NE + 48
FIRST_VSLOT = (0, 24, 40)
GROUP = 8
VMEM_LIMIT = 28 * 1024 * 1024
F32 = jnp.float32
BF16 = jnp.bfloat16
HIGHEST = lax.Precision.HIGHEST

ANY = pl.BlockSpec(memory_space=pl.ANY)
VM = pl.BlockSpec(memory_space=pltpu.VMEM)
SM = pl.BlockSpec(memory_space=pltpu.SMEM)


def on_chip(x):
    return pltpu.with_memory_space_constraint(x, pltpu.VMEM)


def pieces(x):
    out = []
    for _ in range(SPLIT - 1):
        part = x.astype(BF16)
        out.append(part)
        x = x - part.astype(F32)
    out.append(x.astype(BF16))
    return out


def convert_kernel(cols_ref, base_ref, h_ref, hs_ref, list_ref, cnt_ref):
    r = pl.program_id(0)

    @pl.when(r == 0)
    def _():
        for p in range(3):
            cnt_ref[p] = 0

    for n in range(NNZB):
        hi, mid, lo = pieces(h_ref[0, n])
        e = r * NNZB + n
        hs_ref[e, 0:BS, :] = hi
        hs_ref[e, BS : 2 * BS, :] = mid
        hs_ref[e, 2 * BS : 3 * BS, :] = lo
        slot = cols_ref[r, n]
        kind = jnp.where(slot < RB, 0, 1 + lax.shift_right_logical(slot - RB, 3))
        v = slot + base_ref[kind]
        phase = (v >= FIRST_VSLOT[1]).astype(jnp.int32) + (v >= FIRST_VSLOT[2]).astype(jnp.int32)
        at = cnt_ref[phase]
        list_ref[phase, at] = r * 65536 + e * 64 + v
        cnt_ref[phase] = at + 1
    for p in range(3):
        at = cnt_ref[p]
        list_ref[p, at] = r * 65536 + VZERO
        cnt_ref[p] = at + (at & 1)

    @pl.when(r == RB - 1)
    def _():
        for p in range(3):
            at = cnt_ref[p]
            for i in range(2 * GROUP):
                list_ref[p, at + i] = VZERO


def convert(hblocks, local_cols, base):
    return pl.pallas_call(
        convert_kernel,
        grid=(RB,),
        in_specs=[SM, SM, pl.BlockSpec((1, NNZB, BS, BS), lambda r: (r, 0, 0, 0))],
        out_specs=[VM, SM, SM],
        out_shape=[
            pltpu.VMEM((NE, SPLIT * BS, BS), BF16),
            jax.ShapeDtypeStruct((3, MAXE), jnp.int32),
            jax.ShapeDtypeStruct((3,), jnp.int32),
        ],
        compiler_params=pltpu.CompilerParams(vmem_limit_bytes=VMEM_LIMIT),
        cost_estimate=pl.CostEstimate(flops=NE * BS * BS * 8, bytes_accessed=NE * BS * BS * 4, transcendentals=0),
        name="convert",
    )(local_cols, base, hblocks)


def pack_kernel(sel_ref, blocks_ref, *outs):
    for t in range(4):
        for g in range(GHOST):
            outs[t][g] = blocks_ref[sel_ref[t, g]]


def pack(sel, blocks):
    return pl.pallas_call(
        pack_kernel,
        in_specs=[SM, VM],
        out_specs=[VM] * 4,
        out_shape=[jax.ShapeDtypeStruct((GHOST, BS, W), F32)] * 4,
        name="pack",
    )(sel, blocks)


def load_table(v12_ref, v3_ref, at, block):
    hi, mid, lo = pieces(block)
    v12_ref[at, :, 0:W] = hi
    v12_ref[at, :, W : 2 * W] = mid
    v3_ref[at] = lo


def products(phase, list_ref, cnt_ref, hs_ref, v12_ref, v3_ref, acc_ref):
    def step(g, carry):
        for i in range(GROUP):
            one = list_ref[phase, g * (2 * GROUP) + 2 * i]
            two = list_ref[phase, g * (2 * GROUP) + 2 * i + 1]
            row = lax.shift_right_logical(one, 16)
            e1 = lax.shift_right_logical(one, 6) & 1023
            e2 = lax.shift_right_logical(two, 6) & 1023
            s1 = one & 63
            s2 = two & 63
            lhs = jnp.concatenate([hs_ref[e1], hs_ref[e2]], axis=1)
            rhs = jnp.concatenate([v12_ref[s1], v12_ref[s2]], axis=0)
            low = jnp.concatenate([v3_ref[s1], v3_ref[s2]], axis=0)
            big = jnp.dot(lhs, rhs, preferred_element_type=F32)
            small = jnp.dot(lhs[0:BS], low, preferred_element_type=F32)
            total = big[0:BS, 0:W] + (
                (big[0:BS, W:] + big[BS : 2 * BS, 0:W]) + (big[BS : 2 * BS, W:] + big[2 * BS :, 0:W] + small)
            )
            acc_ref[row] = acc_ref[row] + total
        return carry

    count = cnt_ref[phase]
    steps = lax.shift_right_logical(count + (2 * GROUP - 1), 4)
    lax.fori_loop(0, steps, step, 0)


def phase_kernel(phase, nbufs, list_ref, cnt_ref, *refs):
    hs_ref = refs[0]
    bufs = refs[1 : 1 + nbufs]
    rest = refs[1 + nbufs :]
    if phase == 0:
        acc_in = None
        acc_ref, v12_ref, v3_ref = rest
        acc_ref[...] = jnp.zeros_like(acc_ref)
    else:
        acc_in, acc_ref, v12_ref, v3_ref = rest
        acc_ref[...] = acc_in[...]
    v12_ref[VZERO] = jnp.zeros((BS, 2 * W), BF16)
    v3_ref[VZERO] = jnp.zeros((BS, W), BF16)
    at = FIRST_VSLOT[phase]
    for buf in bufs:
        for i in range(buf.shape[0]):
            load_table(v12_ref, v3_ref, at, buf[i])
            at += 1
    products(phase, list_ref, cnt_ref, hs_ref, v12_ref, v3_ref, acc_ref)


TABLE = [pltpu.VMEM((VZERO + 1, BS, 2 * W), BF16), pltpu.VMEM((VZERO + 1, BS, W), BF16)]


def run_phase(phase, lists, cnt, hs, bufs, acc):
    args = [lists, cnt, on_chip(hs), *bufs] + ([] if acc is None else [acc])
    share = (24, 16, 8)[phase] / 48
    return pl.pallas_call(
        functools.partial(phase_kernel, phase, len(bufs)),
        in_specs=[SM, SM] + [VM] * (len(args) - 2),
        out_specs=VM,
        out_shape=jax.ShapeDtypeStruct((RB, BS, W), F32),
        scratch_shapes=TABLE,
        compiler_params=pltpu.CompilerParams(vmem_limit_bytes=VMEM_LIMIT),
        cost_estimate=pl.CostEstimate(
            flops=int(NE * share * 2 * 6 * BS**3), bytes_accessed=4 * 2**20, transcendentals=0
        ),
        name=f"phase{phase}",
    )(*args)


def finish_one_kernel(list_ref, cnt_ref, sel_ref, hs_ref, buf_ref, acc_in, v_ref, first_ref, *rest):
    outs, (v12_ref, v3_ref) = rest[:4], rest[4:]
    first_ref[...] = acc_in[...] - 0.5 * v_ref[...]
    v12_ref[VZERO] = jnp.zeros((BS, 2 * W), BF16)
    v3_ref[VZERO] = jnp.zeros((BS, W), BF16)
    for i in range(GHOST):
        load_table(v12_ref, v3_ref, FIRST_VSLOT[2] + i, buf_ref[i])
    products(2, list_ref, cnt_ref, hs_ref, v12_ref, v3_ref, first_ref)
    for t in range(4):
        for g in range(GHOST):
            outs[t][g] = first_ref[sel_ref[t, g]]


def finish_one(lists, cnt, sel, hs, buf, acc, v):
    return pl.pallas_call(
        finish_one_kernel,
        in_specs=[SM, SM, SM] + [VM] * 4,
        out_specs=[VM] * 5,
        out_shape=[jax.ShapeDtypeStruct((RB, BS, W), F32)] + [jax.ShapeDtypeStruct((GHOST, BS, W), F32)] * 4,
        scratch_shapes=TABLE,
        compiler_params=pltpu.CompilerParams(vmem_limit_bytes=VMEM_LIMIT),
        cost_estimate=pl.CostEstimate(flops=NE * 2 * BS**3, bytes_accessed=8 * 2**20, transcendentals=0),
        name="finish_one",
    )(lists, cnt, sel, on_chip(hs), buf, acc, v)


def two_sum(a, b):
    s = a + b
    t = s - a
    return s, (a - (s - t)) + (b - t)


def pair_add(ah, al, bh, bl):
    s, e = two_sum(ah, bh)
    e = e + (al + bl)
    h = s + e
    return h, e - (h - s)


def power_scale(biggest):
    q = jnp.full_like(biggest, 2.0**-100)
    qi = jnp.full_like(biggest, 2.0**100)
    for e in (64, 64, 32, 16, 8, 4, 2, 1):
        t = q * (2.0**e)
        up = t <= biggest
        q = jnp.where(up, t, q)
        qi = jnp.where(up, qi * (2.0**-e), qi)
    return q * 2.0, qi * 0.5


def digits(x, bits, count):
    out = []
    x = x * (2.0 ** (bits - 1))
    for i in range(count):
        d = jnp.round(x)
        out.append(d.astype(BF16))
        x = (x - d) * (2.0**bits)
    return out


def gram_of_digits(cols, bits):
    count = len(cols)
    stacked = jnp.concatenate(cols, axis=1)
    full = lax.dot_general(stacked, stacked, (((0,), (0,)), ((), ())), preferred_element_type=F32)
    terms = []
    for w in range(2, 2 * count + 1):
        for i in range(1, count + 1):
            j = w - i
            if 1 <= j <= count:
                block = full[(i - 1) * W : i * W, (j - 1) * W : j * W]
                terms.append(block * (2.0 ** (2 - bits * w)))
    return terms


def finish_two_kernel(list_ref, cnt_ref, hs_ref, buf_ref, acc_in, first_ref, v_ref, out_ref, gram_ref, v12_ref, v3_ref, acc_ref):
    acc_ref[...] = acc_in[...]
    v12_ref[VZERO] = jnp.zeros((BS, 2 * W), BF16)
    v3_ref[VZERO] = jnp.zeros((BS, W), BF16)
    for i in range(GHOST):
        load_table(v12_ref, v3_ref, FIRST_VSLOT[2] + i, buf_ref[i])
    products(2, list_ref, cnt_ref, hs_ref, v12_ref, v3_ref, acc_ref)
    biggest = jnp.zeros((BS, W), F32)
    for r in range(RB):
        second = 2.0 * (acc_ref[r] - 0.5 * first_ref[r]) - v_ref[r]
        out_ref[r] = second
        biggest = jnp.maximum(biggest, jnp.abs(second))
    biggest = jnp.max(biggest, axis=0, keepdims=True)
    scale, inverse = power_scale(jnp.broadcast_to(biggest, (8, W)))
    scaled = out_ref[...].reshape(RB * BS, W) * inverse[0:1]
    terms = gram_of_digits(digits(scaled, 7, 4), 7)
    hi = terms[0]
    lo = jnp.zeros_like(hi)
    for t in terms[1:]:
        hi, e = two_sum(hi, t)
        lo = lo + e
    wide = jnp.broadcast_to(scale[0:1], (W, W))
    both = wide.T
    gram_ref[0] = (hi * wide) * both
    gram_ref[1] = (lo * wide) * both


def finish_two(lists, cnt, hs, buf, acc, first, v):
    return pl.pallas_call(
        finish_two_kernel,
        in_specs=[SM, SM] + [VM] * 5,
        out_specs=[VM] * 2,
        out_shape=[jax.ShapeDtypeStruct((RB, BS, W), F32), jax.ShapeDtypeStruct((2, W, W), F32)],
        scratch_shapes=TABLE + [pltpu.VMEM((RB, BS, W), F32)],
        compiler_params=pltpu.CompilerParams(vmem_limit_bytes=VMEM_LIMIT),
        cost_estimate=pl.CostEstimate(flops=NE * 2 * BS**3, bytes_accessed=8 * 2**20, transcendentals=0),
        name="finish_two",
    )(lists, cnt, on_chip(hs), buf, acc, first, v)


def eliminate(A):
    ri = lax.broadcasted_iota(jnp.int32, (8, W), 0)
    ci = lax.broadcasted_iota(jnp.int32, (8, W), 1)
    nb = W // 8
    A = [A[8 * b : 8 * b + 8, :] for b in range(nb)]
    B = [(ci == ri + 8 * b).astype(F32) for b in range(nb)]
    for j in range(W):
        bj, r = divmod(j, 8)
        row = jnp.broadcast_to(A[bj][r : r + 1, :], (8, W))
        brow = jnp.broadcast_to(B[bj][r : r + 1, :], (8, W))
        inv = 1.0 / jnp.broadcast_to(row[:, j : j + 1], (8, W))
        srow = row * inv
        sbrow = brow * inv
        for b in range(bj, nb):
            if b == bj and r == 7:
                continue
            col = jnp.broadcast_to(A[b][:, j : j + 1], (8, W))
            if b == bj:
                col = jnp.where(ri > r, col, 0.0)
            A[b] = A[b] - col * srow
            B[b] = B[b] - col * sbrow
    upper, lower_inv = [], []
    for b in range(nb):
        diag = jnp.sum(jnp.where(ci == ri + 8 * b, A[b], 0.0), axis=1, keepdims=True)
        s = 1.0 / jnp.sqrt(diag)
        upper.append(jnp.where(ci >= ri + 8 * b, A[b] * s, 0.0))
        lower_inv.append(jnp.where(ci <= ri + 8 * b, B[b] * s, 0.0))
    return jnp.concatenate(upper, axis=0), jnp.concatenate(lower_inv, axis=0)


def mm(a, b):
    return jnp.dot(a, b, precision=HIGHEST, preferred_element_type=F32)


def factor_kernel(total, gram_ref, inv_ref, factor_ref, u_ref, x_ref, y_ref):
    ri = lax.broadcasted_iota(jnp.int32, (W, W), 0)
    ci = lax.broadcasted_iota(jnp.int32, (W, W), 1)
    eye = (ri == ci).astype(F32)
    hi = gram_ref[0] * (1.0 / total)
    lo = gram_ref[1] * (1.0 / total)
    upper, linv = eliminate(hi)

    biggest = jnp.max(jnp.abs(upper), axis=0, keepdims=True)
    scale, inverse = power_scale(jnp.broadcast_to(biggest, (8, W)))
    wide, wide_inv = jnp.broadcast_to(scale[0:1], (W, W)), jnp.broadcast_to(inverse[0:1], (W, W))
    tall, tall_inv = wide.T, wide_inv.T
    rest = (hi * wide_inv) * tall_inv
    small = (lo * wide_inv) * tall_inv
    for t in gram_of_digits(digits(upper * wide_inv, 8, 4), 8):
        rest, e = two_sum(rest, -t)
        small = small + e
    rest = ((rest + small) * wide) * tall

    off = mm(mm(linv, rest), linv.T)
    off = 0.5 * (off + off.T)
    norm = jnp.sum(off * off)

    def half_lower(x):
        return jnp.where(ri > ci, x, jnp.where(ri == ci, 0.5 * x, 0.0))

    close = norm < 1e-5

    @pl.when(close)
    def _():
        x = half_lower(off)
        for _ in range(2):
            x = half_lower(off - mm(x, x.T))
        x_ref[...] = eye + x
        y_ref[...] = mm(eye - x, eye + mm(x, x))

    @pl.when(jnp.logical_not(close))
    def _():
        u2, l2 = eliminate(eye + off)
        x_ref[...] = u2.T
        y_ref[...] = l2

    upper_two = x_ref[...].T
    factor = mm(upper_two, upper)
    inv = mm(y_ref[...], linv).T
    inv = inv + mm(inv, eye - mm(factor, inv))
    inv_ref[...] = jnp.where(ri <= ci, inv, 0.0)
    factor_ref[...] = factor


def factors(gram, total):
    return pl.pallas_call(
        functools.partial(factor_kernel, float(total)),
        in_specs=[VM],
        out_specs=[VM, VM],
        out_shape=[jax.ShapeDtypeStruct((W, W), F32)] * 2,
        scratch_shapes=[pltpu.VMEM((W, W), F32)] * 3,
        compiler_params=pltpu.CompilerParams(vmem_limit_bytes=VMEM_LIMIT),
        name="factors",
    )(gram)


def basis_kernel(s_ref, t_ref, out_ref):
    out_ref[...] = mm(s_ref[...], t_ref[...])


def basis_of(second, inv):
    rows = second.shape[0]
    part = rows // 4
    return pl.pallas_call(
        basis_kernel,
        grid=(4,),
        in_specs=[pl.BlockSpec((part, W), lambda i: (i, 0)), pl.BlockSpec((W, W), lambda i: (0, 0))],
        out_specs=pl.BlockSpec((part, W), lambda i: (i, 0)),
        out_shape=jax.ShapeDtypeStruct((rows, W), F32),
        name="basis",
    )(second, inv)


def shards(vectors, hblocks, local_cols, ghost_lists):
    count = lax.axis_size("rows")
    me = lax.axis_index("rows")
    chips = count // 2
    core = me % 2
    odd = (me // 2) % 2

    def to_chip(i, by):
        return ((i // 2 + by) % chips) * 2 + i % 2

    pair_c = [(i, i ^ 1) for i in range(count)]
    pair_a = [(i, to_chip(i, 1 if (i // 2) % 2 == 0 else -1)) for i in range(count)]
    pair_b = [(i, to_chip(i, -1 if (i // 2) % 2 == 0 else 1)) for i in range(count)]
    pair_d = [(i, (i + (1 if i % 2 else -1)) % count) for i in range(count)]

    mine = lax.dynamic_index_in_dim(ghost_lists, me, 0, keepdims=False)
    which = jnp.stack([1 + core, 3 * odd, 3 - 3 * odd, 2 - core])
    sel = mine[which]
    at_c, at_a, at_b, at_d = 16, 24, 32, 40
    base = jnp.stack(
        [
            jnp.zeros_like(me),
            jnp.where(odd == 1, at_a, at_b) - 16,
            jnp.where(core == 1, at_c, at_d) - 24,
            jnp.where(core == 1, at_d, at_c) - 32,
            jnp.where(odd == 1, at_b, at_a) - 40,
        ]
    ).astype(jnp.int32)

    v = vectors.reshape(RB, BS, W)
    move = functools.partial(lax.ppermute, axis_name="rows")

    def gather(packs, hold):
        c = move(packs[0], perm=pair_c)
        a = move(packs[1], perm=pair_a)
        b = move(packs[2], perm=pair_b)
        return c, a, b

    packs = pack(sel, v)
    c, a, b = gather(packs, None)
    hs, lists, cnt = convert(hblocks, local_cols, base)
    d = move(packs[3], perm=pair_d)
    acc = run_phase(0, lists, cnt, hs, [v, c], None)
    acc = run_phase(1, lists, cnt, hs, [a, b], acc)
    first, *packs = finish_one(lists, cnt, sel, hs, d, acc, v)

    c, a, b = gather(packs, None)
    d = move(packs[3], perm=pair_d)
    acc = run_phase(0, lists, cnt, hs, [first, c], None)
    acc = run_phase(1, lists, cnt, hs, [a, b], acc)
    second, gram = finish_two(lists, cnt, hs, d, acc, first, v)

    perms = [[(i, i ^ 1) for i in range(count)]]
    for shift in (1, 3, 5):
        def flip(i, by):
            return i ^ (by << shift)

        perms.append([(i, flip(i, 1)) for i in range(count)])
        perms.append([(i, flip(i, 3)) for i in range(count)])
    hi, lo = gram[0], gram[1]
    for perm in perms:
        theirs = move(jnp.stack([hi, lo]), perm=perm)
        hi, lo = pair_add(hi, lo, theirs[0], theirs[1])
    inv, factor = factors(jnp.stack([hi, lo]), RB * BS * count)
    return basis_of(second.reshape(RB * BS, W), inv), factor


def solution(mesh):
    in_specs = (P("rows", None), P("rows", None, None, None), P("rows", None), P())
    out_specs = (P("rows", None), P())
    return jax.shard_map(shards, mesh=mesh, in_specs=in_specs, out_specs=out_specs, check_vma=False)
```

```python
import functools

import jax
import jax.numpy as jnp
from jax import lax
from jax.experimental import pallas as pl
from jax.experimental.pallas import tpu as pltpu
from jax.sharding import PartitionSpec as P

BS = 128
W = 128
RB = 16
GHOST = 8
NNZB = 20
NE = RB * NNZB
SPLIT = 3
BAND = W // 4
PACKED = BAND + 8
A_B_D = 4
VZERO = 48
MAXE = NE + 48
OWN, AT_C, AT_A, AT_B, AT_D = 0, 16, 24, 32, 40
LISTS = 5
GROUP = 8
FETCH, FETCHES = 10, 8
VMEM_LIMIT = 26 * 1024 * 1024
F32 = jnp.float32
BF16 = jnp.bfloat16
HIGHEST = lax.Precision.HIGHEST

ANY = pl.BlockSpec(memory_space=pl.ANY)
VM = pl.BlockSpec(memory_space=pltpu.VMEM)
SM = pl.BlockSpec(memory_space=pltpu.SMEM)


def on_chip(x):
    return pltpu.with_memory_space_constraint(x, pltpu.VMEM)


def pieces(x, count=SPLIT):
    out = []
    for _ in range(count - 1):
        part = x.astype(BF16)
        out.append(part)
        x = x - part.astype(F32)
    out.append(x.astype(BF16))
    return out


def load_table(v12_ref, v3_ref, at, block):
    hi, mid, lo = pieces(block)
    v12_ref[at, :, 0:W] = hi
    v12_ref[at, :, W : 2 * W] = mid
    v3_ref[at] = lo


def load_zero(v12_ref, v3_ref):
    v12_ref[VZERO] = jnp.zeros((BS, 2 * W), BF16)
    v3_ref[VZERO] = jnp.zeros((BS, W), BF16)


def group_of_products(which, first, count, list_ref, hs_ref, v12_ref, v3_ref, acc_ref):
    for i in range(count):
        one = list_ref[which, first + 2 * i]
        two = list_ref[which, first + 2 * i + 1]
        row = lax.shift_right_logical(one, 16)
        e1 = lax.shift_right_logical(one, 6) & 1023
        e2 = lax.shift_right_logical(two, 6) & 1023
        s1 = one & 63
        s2 = two & 63
        lhs = jnp.concatenate([hs_ref[e1], hs_ref[e2]], axis=1)
        rhs = jnp.concatenate([v12_ref[s1], v12_ref[s2]], axis=0)
        low = jnp.concatenate([v3_ref[s1], v3_ref[s2]], axis=0)
        big = jnp.dot(lhs, rhs, preferred_element_type=F32)
        small = jnp.dot(lhs[0:BS], low, preferred_element_type=F32)
        total = big[0:BS, 0:W] + (
            (big[0:BS, W:] + big[BS : 2 * BS, 0:W]) + (big[BS : 2 * BS, W:] + big[2 * BS :, 0:W] + small)
        )
        acc_ref[row] = acc_ref[row] + total


def products(which, group, list_ref, cnt_ref, *refs):
    def large(g, carry):
        group_of_products(which, g * (2 * group), group, list_ref, *refs)
        return carry

    def small(g, carry):
        group_of_products(which, begin + g * (2 * GROUP), GROUP, list_ref, *refs)
        return carry

    count = cnt_ref[which]
    begin = 0
    if group > GROUP:
        steps = lax.div(count, 2 * group)
        lax.fori_loop(0, steps, large, 0)
        begin = steps * (2 * group)
    lax.fori_loop(0, lax.div(count - begin + (2 * GROUP - 1), 2 * GROUP), small, 0)


def convert_kernel(cols_ref, info_ref, h_ref, hs_ref, list_ref, cnt_ref, buf_ref, sem_ref):
    def fetch(i, slot):
        return pltpu.make_async_copy(h_ref.at[pl.ds(i * FETCH, FETCH)], buf_ref.at[slot], sem_ref.at[slot])

    for i in range(FETCHES):
        fetch(i, i).start()
    def list_row(r, counts):
        counts = list(counts)
        for n in range(NNZB):
            col = cols_ref[r, n]
            kind = jnp.where(col < RB, 0, 1 + lax.shift_right_logical(col - RB, 3))
            v = col + info_ref[4 + kind]
            code = r * 65536 + (r * NNZB + n) * 64 + v
            source = lax.shift_right_logical(v, 3)
            mine = [source < 3, source == 3, source == 4, source == 5]
            at = jnp.where(mine[0], counts[0], jnp.where(mine[1], counts[1], jnp.where(mine[2], counts[2], counts[3])))
            list_ref[jnp.maximum(source - 2, 0), at] = code
            list_ref[A_B_D, counts[4]] = code
            for p, yes in enumerate((*mine, source >= 3)):
                counts[p] = counts[p] + yes.astype(jnp.int32)
        for p in range(LISTS):
            list_ref[p, counts[p]] = r * 65536 + VZERO
            counts[p] = counts[p] + (counts[p] & 1)
        return tuple(counts)

    counts = lax.fori_loop(0, RB, list_row, (jnp.int32(0),) * LISTS)
    for p in range(LISTS):
        cnt_ref[p] = counts[p]
        for i in range(2 * GROUP):
            list_ref[p, counts[p] + i] = VZERO

    def part(i, carry):
        slot = lax.rem(i, FETCHES)
        fetch(i, slot).wait()
        for n in range(FETCH):
            e = i * FETCH + n
            hi, mid, lo = pieces(buf_ref[slot, n])
            hs_ref[e, 0:BS, :] = hi
            hs_ref[e, BS : 2 * BS, :] = mid
            hs_ref[e, 2 * BS : 3 * BS, :] = lo

        @pl.when(i + FETCHES < NE // FETCH)
        def _():
            fetch(i + FETCHES, slot).start()

        return carry

    lax.fori_loop(0, NE // FETCH, part, 0)


TABLE = [pltpu.VMEM((VZERO + 1, BS, 2 * W), BF16), pltpu.VMEM((VZERO + 1, BS, W), BF16)]


def convert(hblocks, local_cols, info):
    return pl.pallas_call(
        convert_kernel,
        in_specs=[SM, SM, ANY],
        out_specs=[VM, SM, SM],
        out_shape=[
            pltpu.VMEM((NE, SPLIT * BS, BS), BF16),
            jax.ShapeDtypeStruct((LISTS, MAXE), jnp.int32),
            jax.ShapeDtypeStruct((LISTS,), jnp.int32),
        ],
        scratch_shapes=[pltpu.VMEM((FETCHES, FETCH, BS, BS), F32), pltpu.SemaphoreType.DMA((FETCHES,))],
        compiler_params=pltpu.CompilerParams(vmem_limit_bytes=VMEM_LIMIT),
        cost_estimate=pl.CostEstimate(flops=NE * 4 * BS**3, bytes_accessed=NE * BS * BS * 4, transcendentals=0),
        name="convert",
    )(local_cols, info, hblocks.reshape(NE, BS, BS))


def fill_packs(info_ref, lists_ref, blocks_ref, outs):
    for t in range(4):
        for g in range(GHOST):
            outs[t][g] = blocks_ref[lists_ref[info_ref[t], g]]


PACKS = [pltpu.VMEM((GHOST, BS, W), F32)] * 4


def pack_kernel(info_ref, lists_ref, v_ref, held_ref, *rest):
    outs, sem_ref = rest[:4], rest[4]
    copies = []
    for i in range(RB // 2):
        part = pl.ds(2 * i, 2)
        copies.append(pltpu.make_async_copy(v_ref.at[part], held_ref.at[part], sem_ref.at[i]))
        copies[-1].start()
    for copy in copies:
        copy.wait()
    fill_packs(info_ref, lists_ref, held_ref, outs)


def pack(info, mine, v):
    return pl.pallas_call(
        pack_kernel,
        in_specs=[SM, SM, pl.BlockSpec(memory_space=pltpu.HBM)],
        out_specs=[VM] * 5,
        out_shape=[pltpu.VMEM((RB, BS, W), F32)] + PACKS,
        scratch_shapes=[pltpu.SemaphoreType.DMA((RB // 2,))],
        compiler_params=pltpu.CompilerParams(vmem_limit_bytes=VMEM_LIMIT),
        name="pack",
    )(info, mine, pltpu.with_memory_space_constraint(v, pltpu.HBM))


def add_list(which, group, places, bufs, list_ref, cnt_ref, hs_ref, v12_ref, v3_ref, acc_ref):
    load_zero(v12_ref, v3_ref)
    for place, buf in zip(places, bufs):
        for i in range(buf.shape[0]):
            load_table(v12_ref, v3_ref, place + i, buf[i])
    products(which, group, list_ref, cnt_ref, hs_ref, v12_ref, v3_ref, acc_ref)


def phase_kernel(which, group, places, fresh, list_ref, cnt_ref, hs_ref, *refs):
    bufs = refs[: len(places)]
    acc_ref, v12_ref, v3_ref = refs[-3:]
    if fresh:
        acc_ref[...] = jnp.zeros_like(acc_ref)
    add_list(which, group, places, bufs, list_ref, cnt_ref, hs_ref, v12_ref, v3_ref, acc_ref)


def run_phase(which, group, places, lists, cnt, hs, bufs, acc=None):
    args = [lists, cnt] + [on_chip(x) for x in (hs, *bufs)] + ([] if acc is None else [on_chip(acc)])
    return pl.pallas_call(
        functools.partial(phase_kernel, which, group, places, acc is None),
        in_specs=[SM, SM] + [VM] * (len(args) - 2),
        out_specs=VM,
        out_shape=pltpu.VMEM((RB, BS, W), F32),
        scratch_shapes=TABLE,
        input_output_aliases={} if acc is None else {len(args) - 1: 0},
        compiler_params=pltpu.CompilerParams(vmem_limit_bytes=VMEM_LIMIT),
        cost_estimate=pl.CostEstimate(
            flops=len(places) * NE * 2 * BS**3, bytes_accessed=4 * 2**20, transcendentals=0
        ),
        name=f"phase_{which}",
    )(*args)


def finish_one_kernel(
    list_ref, cnt_ref, info_ref, mine_ref, hs_ref, a_ref, b_ref, d_ref, v_ref, acc_in, first_ref, *rest
):
    outs, tables = rest[:4], rest[4:]
    for r in range(RB):
        first_ref[r] = first_ref[r] - 0.5 * v_ref[r]
    places, bufs = (AT_A, AT_B, AT_D), (a_ref, b_ref, d_ref)
    add_list(A_B_D, 2 * GROUP, places, bufs, list_ref, cnt_ref, hs_ref, *tables, first_ref)
    fill_packs(info_ref, mine_ref, first_ref, outs)


def finish_one(lists, cnt, info, mine, hs, bufs, v, acc):
    return pl.pallas_call(
        finish_one_kernel,
        in_specs=[SM] * 4 + [VM] * 6,
        out_specs=[VM] * 5,
        out_shape=[pltpu.VMEM((RB, BS, W), F32)] + PACKS,
        scratch_shapes=TABLE,
        input_output_aliases={9: 0},
        compiler_params=pltpu.CompilerParams(vmem_limit_bytes=VMEM_LIMIT),
        cost_estimate=pl.CostEstimate(flops=NE * 6 * BS**3, bytes_accessed=8 * 2**20, transcendentals=0),
        name="finish_one",
    )(lists, cnt, info, mine, on_chip(hs), *[on_chip(x) for x in bufs], on_chip(v), on_chip(acc))


def two_sum(a, b):
    s = a + b
    t = s - a
    return s, (a - (s - t)) + (b - t)


def pair_add(ah, al, bh, bl):
    s, e = two_sum(ah, bh)
    e = e + (al + bl)
    h = s + e
    return h, e - (h - s)


def power_scale(biggest):
    q = jnp.full_like(biggest, 2.0**-100)
    qi = jnp.full_like(biggest, 2.0**100)
    for e in (64, 64, 32, 16, 8, 4, 2, 1):
        t = q * (2.0**e)
        up = t <= biggest
        q = jnp.where(up, t, q)
        qi = jnp.where(up, qi * (2.0**-e), qi)
    return q * 2.0, qi * 0.5


def digits(x, bits, count):
    out = []
    x = x * (2.0 ** (bits - 1))
    for i in range(count):
        d = jnp.round(x)
        out.append(d.astype(BF16))
        x = (x - d) * (2.0**bits)
    return out


def gram_of_digits(cols, bits):
    count = len(cols)
    stacked = jnp.concatenate(cols, axis=1)
    full = lax.dot_general(stacked, stacked, (((0,), (0,)), ((), ())), preferred_element_type=F32)
    terms = []
    for w in range(2, 2 * count):
        total = None
        for i in range(1, count + 1):
            j = w - i
            if 1 <= j <= count:
                block = full[(i - 1) * W : i * W, (j - 1) * W : j * W]
                total = block if total is None else total + block
        terms.append(total * (2.0 ** (2 - bits * w)))
    return terms


def lanes_of(rows):
    return lax.broadcasted_iota(jnp.int32, (rows, W), 1)


def pack_symmetric(g):
    lane = lanes_of(BAND)
    small = lanes_of(8)

    def tail(at):
        out = jnp.zeros((8, W), F32)
        for q in range(4):
            moved = pltpu.roll(g[at + 8 * q : at + 8 * q + 8], (BAND * q - at) % W, 1)
            out = jnp.where(lax.shift_right_logical(small, 5) == q, moved, out)
        return out

    zero = jnp.where(lane < 3 * BAND, g[0:BAND], g[2 * BAND : 3 * BAND])
    one = jnp.where(lane >= BAND, g[BAND : 2 * BAND], g[3 * BAND :])
    return jnp.concatenate([zero, tail(2 * BAND)], axis=0), jnp.concatenate([one, tail(3 * BAND)], axis=0)


def unpack_symmetric(zero, one):
    lane = lanes_of(BAND)

    def tail(packed, at):
        return jnp.concatenate([pltpu.roll(packed[BAND:], (at - BAND * q) % W, 1) for q in range(4)], axis=0)

    two = jnp.where(lane >= 3 * BAND, zero[0:BAND], tail(zero, 2 * BAND))
    three = jnp.where(lane < BAND, one[0:BAND], tail(one, 3 * BAND))
    half = jnp.concatenate([zero[0:BAND], one[0:BAND], two, three], axis=0)
    i = lax.shift_right_logical(lax.broadcasted_iota(jnp.int32, (W, W), 0), 5)
    j = lax.shift_right_logical(lax.broadcasted_iota(jnp.int32, (W, W), 1), 5)
    ahead = (j - i) & 3
    return jnp.where((ahead < 2) | ((ahead == 2) & (i < 2)), half, half.T)


def finish_two_kernel(
    list_ref, cnt_ref, info_ref, hs_ref, buf_ref, first_ref, v_ref, acc_in,
    out_ref, keep_ref, send_ref, v12_ref, v3_ref,
):
    add_list(3, GROUP, (AT_D,), (buf_ref,), list_ref, cnt_ref, hs_ref, v12_ref, v3_ref, out_ref)
    biggest = jnp.zeros((BS, W), F32)
    for r in range(RB):
        second = 2.0 * (out_ref[r] - 0.5 * first_ref[r]) - v_ref[r]
        out_ref[r] = second
        biggest = jnp.maximum(biggest, jnp.abs(second))
    biggest = jnp.max(biggest, axis=0, keepdims=True)
    scale, inverse = power_scale(jnp.broadcast_to(biggest, (8, W)))
    scaled = out_ref[...].reshape(RB * BS, W) * inverse[0:1]
    terms = gram_of_digits(digits(scaled, 7, 4), 7)
    hi = terms[0]
    lo = jnp.zeros_like(hi)
    for t in terms[1:]:
        hi, e = two_sum(hi, t)
        lo = lo + e
    wide = jnp.broadcast_to(scale[0:1], (W, W))
    both = wide.T
    core = info_ref[9]
    for i, part in enumerate((hi, lo)):
        zero, one = pack_symmetric((part * wide) * both)
        keep_ref[i] = jnp.where(core == 0, zero, one)
        send_ref[i] = jnp.where(core == 0, one, zero)


def finish_two(lists, cnt, info, hs, buf, first, v, acc):
    return pl.pallas_call(
        finish_two_kernel,
        in_specs=[SM] * 3 + [VM] * 5,
        out_specs=[VM] * 3,
        out_shape=[pltpu.VMEM((RB, BS, W), F32)] + [pltpu.VMEM((2, PACKED, W), F32)] * 2,
        scratch_shapes=TABLE,
        input_output_aliases={7: 0},
        compiler_params=pltpu.CompilerParams(vmem_limit_bytes=VMEM_LIMIT),
        cost_estimate=pl.CostEstimate(flops=NE * 2 * BS**3, bytes_accessed=8 * 2**20, transcendentals=0),
        name="finish_two",
    )(lists, cnt, info, on_chip(hs), on_chip(buf), on_chip(first), on_chip(v), on_chip(acc))


def eliminate(G):
    ri = lax.broadcasted_iota(jnp.int32, (8, W), 0)
    ci = lax.broadcasted_iota(jnp.int32, (8, W), 1)
    nb = W // 8
    A = [G[8 * b : 8 * b + 8, :] for b in range(nb)]
    B = [(ci == ri + 8 * b).astype(F32) for b in range(nb)]
    upper, lower_inv = [], []
    for k in range(nb):
        lanes = [jnp.broadcast_to(A[k][:, 8 * k + c : 8 * k + c + 1], (8, W)) for c in range(8)]
        d = [[jnp.broadcast_to(lanes[c][m : m + 1, :], (8, W)) for c in range(m + 1)] for m in range(8)]
        ra = [jnp.broadcast_to(A[k][m : m + 1, :], (8, W)) for m in range(8)]
        rb = [jnp.broadcast_to(B[k][m : m + 1, :], (8, W)) for m in range(8)]
        cols = {b: [jnp.broadcast_to(A[b][:, 8 * k + c : 8 * k + c + 1], (8, W)) for c in range(8)] for b in range(k + 1, nb)}
        inv = [None] * 8
        l = [[None] * 8 for _ in range(8)]
        for i in range(8):
            inv[i] = 1.0 / d[i][i]
            for m in range(i + 1, 8):
                l[m][i] = d[m][i] * inv[i]
                for c in range(i + 1, m + 1):
                    d[m][c] = d[m][c] - l[m][i] * d[c][i]
            for m in range(i + 1, 8):
                ra[m] = ra[m] - l[m][i] * ra[i]
                rb[m] = rb[m] - l[m][i] * rb[i]
        sa = [ra[i] * inv[i] for i in range(8)]
        sb = [rb[i] * inv[i] for i in range(8)]
        for b in range(k + 1, nb):
            c = cols[b]
            for i in range(8):
                for j in range(i):
                    c[i] = c[i] - l[i][j] * c[j]
                A[b] = A[b] - c[i] * sa[i]
                B[b] = B[b] - c[i] * sb[i]
        pa, pb, pd = ra[0], rb[0], d[0][0]
        for m in range(1, 8):
            pa = jnp.where(ri == m, ra[m], pa)
            pb = jnp.where(ri == m, rb[m], pb)
            pd = jnp.where(ri == m, d[m][m], pd)
        s = 1.0 / jnp.sqrt(pd)
        upper.append(jnp.where(ci >= ri + 8 * k, pa * s, 0.0))
        lower_inv.append(jnp.where(ci <= ri + 8 * k, pb * s, 0.0))
    return jnp.concatenate(upper, axis=0), jnp.concatenate(lower_inv, axis=0)


def dot(a, b, ca, cb):
    return lax.dot_general(a, b, (((ca,), (cb,)), ((), ())), preferred_element_type=F32)


def mm1(a, b, ca=1, cb=0):
    return dot(a.astype(BF16), b.astype(BF16), ca, cb)


def mm3(a, b, ca=1, cb=0):
    ah, al = pieces(a, 2)
    bh, bl = pieces(b, 2)
    return dot(jnp.concatenate([al, ah, ah], axis=ca), jnp.concatenate([bh, bl, bh], axis=cb), ca, cb)


def mm6(a, b, ca=1, cb=0):
    ah, am, al = pieces(a)
    bh, bm, bl = pieces(b)
    return dot(
        jnp.concatenate([al, ah, am, am, ah, ah], axis=ca), jnp.concatenate([bh, bl, bm, bh, bm, bh], axis=cb), ca, cb
    )


def factor_kernel(total, info_ref, kept_ref, other_ref, inv_ref, factor_ref):
    ri = lax.broadcasted_iota(jnp.int32, (W, W), 0)
    ci = lax.broadcasted_iota(jnp.int32, (W, W), 1)
    eye = (ri == ci).astype(F32)

    def half_lower(x):
        return jnp.where(ri > ci, x, jnp.where(ri == ci, 0.5 * x, 0.0))

    core = info_ref[9]
    hi, lo = [
        unpack_symmetric(
            jnp.where(core == 0, kept_ref[i], other_ref[i]), jnp.where(core == 0, other_ref[i], kept_ref[i])
        )
        * (1.0 / total)
        for i in range(2)
    ]
    upper, linv = eliminate(hi)

    norm = jnp.sqrt(jnp.sum(hi * eye, axis=0, keepdims=True))
    scale, inverse = power_scale(jnp.broadcast_to(norm, (8, W)))
    wide, wide_inv = jnp.broadcast_to(scale[0:1], (W, W)), jnp.broadcast_to(inverse[0:1], (W, W))
    tall, tall_inv = wide.T, wide_inv.T
    rest = (hi * wide_inv) * tall_inv
    small = (lo * wide_inv) * tall_inv
    for t in gram_of_digits(digits(upper * wide_inv, 8, 4), 8):
        rest, e = two_sum(rest, -t)
        small = small + e
    rest = ((rest + small) * wide) * tall

    off = mm3(mm3(linv, rest), linv, 1, 1)
    defect = eye - mm6(linv, upper, 1, 1)
    close = jnp.sum(off * off) < 1e-5

    @pl.when(close)
    def _():
        x = half_lower(off)
        z = mm1(x, x - defect) + defect
        x = half_lower(off - mm1(x, x, 1, 1))
        inv_ref[...] = linv + mm3(z - x, linv)
        factor_ref[...] = upper + mm3(x, upper, 0, 0)

    @pl.when(jnp.logical_not(close))
    def _():
        u2, l2 = eliminate(eye + off)
        factor = mm6(u2, upper)
        inv = mm6(l2, linv)
        inv_ref[...] = inv + mm6(eye - mm6(inv, factor, 1, 1), inv)
        factor_ref[...] = factor


def factors(info, kept, other, total):
    return pl.pallas_call(
        functools.partial(factor_kernel, float(total)),
        in_specs=[SM, VM, VM],
        out_specs=[VM, VM],
        out_shape=[pltpu.VMEM((W, W), F32), jax.ShapeDtypeStruct((W, W), F32)],
        compiler_params=pltpu.CompilerParams(vmem_limit_bytes=VMEM_LIMIT),
        name="factors",
    )(info, kept, other)


def basis_kernel(s_ref, t_ref, out_ref):
    i = pl.program_id(0)
    out_ref[...] = mm6(s_ref[pl.ds(i * 4, 4)].reshape(4 * BS, W), t_ref[...], 1, 1)


def basis_of(second, inv):
    return pl.pallas_call(
        basis_kernel,
        grid=(RB // 4,),
        in_specs=[VM, VM],
        out_specs=pl.BlockSpec((4 * BS, W), lambda i: (i, 0)),
        out_shape=jax.ShapeDtypeStruct((RB * BS, W), F32),
        compiler_params=pltpu.CompilerParams(vmem_limit_bytes=VMEM_LIMIT),
        name="basis",
    )(on_chip(second), on_chip(inv))


def shards(vectors, hblocks, local_cols, ghost_lists):
    count = lax.axis_size("rows")
    me = lax.axis_index("rows")
    chips = count // 2
    core = me % 2
    odd = (me // 2) % 2

    def to_chip(i, by):
        return ((i // 2 + by) % chips) * 2 + i % 2

    pair_c = [(i, i ^ 1) for i in range(count)]
    pair_a = [(i, to_chip(i, 1 if (i // 2) % 2 == 0 else -1)) for i in range(count)]
    pair_b = [(i, to_chip(i, -1 if (i // 2) % 2 == 0 else 1)) for i in range(count)]
    pair_d = [(i, (i + (1 if i % 2 else -1)) % count) for i in range(count)]

    mine = lax.dynamic_index_in_dim(ghost_lists, me, 0, keepdims=False)
    info = jnp.stack(
        [
            1 + core,
            3 * odd,
            3 - 3 * odd,
            2 - core,
            jnp.zeros_like(me),
            jnp.where(odd == 1, AT_A, AT_B) - 16,
            jnp.where(core == 1, AT_C, AT_D) - 24,
            jnp.where(core == 1, AT_D, AT_C) - 32,
            jnp.where(odd == 1, AT_B, AT_A) - 40,
            core,
        ]
    ).astype(jnp.int32)

    v = vectors.reshape(RB, BS, W)
    move = functools.partial(lax.ppermute, axis_name="rows")

    def exchange(packs):
        return [move(x, perm=perm) for x, perm in zip(packs, (pair_c, pair_a, pair_b, pair_d))]

    v, *packs = pack(info, mine, v)
    c, a, b, d = exchange(packs)
    hs, lists, cnt = convert(hblocks, local_cols, info)
    acc = run_phase(0, 2 * GROUP, (OWN, AT_C), lists, cnt, hs, [v, c])
    first, *packs = finish_one(lists, cnt, info, mine, hs, [a, b, d], v, acc)

    c, a, b, d = exchange(packs)
    acc = run_phase(0, 2 * GROUP, (OWN, AT_C), lists, cnt, hs, [first, c])
    acc = run_phase(1, GROUP, (AT_A,), lists, cnt, hs, [a], acc)
    acc = run_phase(2, GROUP, (AT_B,), lists, cnt, hs, [b], acc)
    second, kept, sent = finish_two(lists, cnt, info, hs, d, first, v, acc)

    theirs = move(sent, perm=pair_c)
    pair = pair_add(kept[0], kept[1], theirs[0], theirs[1])
    for shift in (1, 3, 5):
        for by in (1, 3):
            theirs = move(jnp.stack(pair), perm=[(i, i ^ (by << shift)) for i in range(count)])
            pair = pair_add(*pair, theirs[0], theirs[1])
    kept = jnp.stack(pair)
    inv, factor = factors(info, kept, move(kept, perm=pair_c), RB * BS * count)
    return basis_of(second, inv), factor


def solution(mesh):
    in_specs = (P("rows", None), P("rows", None, None, None), P("rows", None), P())
    out_specs = (P("rows", None), P())
    return jax.shard_map(shards, mesh=mesh, in_specs=in_specs, out_specs=out_specs, check_vma=False)
```

```python
import functools

import jax
import jax.numpy as jnp
from jax import lax
from jax.experimental import pallas as pl
from jax.experimental.pallas import tpu as pltpu
from jax.sharding import PartitionSpec as P

BS = 128
W = 128
RB = 16
GHOST = 8
NNZB = 20
NE = RB * NNZB
SPLIT = 3
BAND = W // 4
PACKED = BAND + 8
A_B_D = 4
VZERO = 48
MAXE = NE + 48
OWN, AT_C, AT_A, AT_B, AT_D = 0, 16, 24, 32, 40
LISTS = 5
GROUP = 8
FETCH, FETCHES = 10, 8
VMEM_LIMIT = 26 * 1024 * 1024
F32 = jnp.float32
BF16 = jnp.bfloat16
HIGHEST = lax.Precision.HIGHEST

ANY = pl.BlockSpec(memory_space=pl.ANY)
VM = pl.BlockSpec(memory_space=pltpu.VMEM)
SM = pl.BlockSpec(memory_space=pltpu.SMEM)


def on_chip(x):
    return pltpu.with_memory_space_constraint(x, pltpu.VMEM)


def pieces(x, count=SPLIT):
    out = []
    for _ in range(count - 1):
        part = x.astype(BF16)
        out.append(part)
        x = x - part.astype(F32)
    out.append(x.astype(BF16))
    return out


def load_table(v12_ref, v3_ref, at, block):
    hi, mid, lo = pieces(block)
    v12_ref[at, :, 0:W] = hi
    v12_ref[at, :, W : 2 * W] = mid
    v3_ref[at] = lo


def load_zero(v12_ref, v3_ref):
    v12_ref[VZERO] = jnp.zeros((BS, 2 * W), BF16)
    v3_ref[VZERO] = jnp.zeros((BS, W), BF16)


def group_of_products(which, first, count, list_ref, hs_ref, v12_ref, v3_ref, acc_ref):
    for i in range(count):
        one = list_ref[which, first + 2 * i]
        two = list_ref[which, first + 2 * i + 1]
        row = lax.shift_right_logical(one, 16)
        e1 = lax.shift_right_logical(one, 6) & 1023
        e2 = lax.shift_right_logical(two, 6) & 1023
        s1 = one & 63
        s2 = two & 63
        lhs = jnp.concatenate([hs_ref[e1], hs_ref[e2]], axis=1)
        rhs = jnp.concatenate([v12_ref[s1], v12_ref[s2]], axis=0)
        low = jnp.concatenate([v3_ref[s1], v3_ref[s2]], axis=0)
        big = jnp.dot(lhs, rhs, preferred_element_type=F32)
        small = jnp.dot(lhs[0:BS], low, preferred_element_type=F32)
        total = big[0:BS, 0:W] + (
            (big[0:BS, W:] + big[BS : 2 * BS, 0:W]) + (big[BS : 2 * BS, W:] + big[2 * BS :, 0:W] + small)
        )
        acc_ref[row] = acc_ref[row] + total


def products(which, group, list_ref, cnt_ref, *refs):
    def large(g, carry):
        group_of_products(which, g * (2 * group), group, list_ref, *refs)
        return carry

    def small(g, carry):
        group_of_products(which, begin + g * (2 * GROUP), GROUP, list_ref, *refs)
        return carry

    count = cnt_ref[which]
    begin = 0
    if group > GROUP:
        steps = lax.div(count, 2 * group)
        lax.fori_loop(0, steps, large, 0)
        begin = steps * (2 * group)
    lax.fori_loop(0, lax.div(count - begin + (2 * GROUP - 1), 2 * GROUP), small, 0)


def convert_kernel(cols_ref, info_ref, h_ref, hs_ref, list_ref, cnt_ref, buf_ref, sem_ref):
    def fetch(i, slot):
        return pltpu.make_async_copy(h_ref.at[pl.ds(i * FETCH, FETCH)], buf_ref.at[slot], sem_ref.at[slot])

    for i in range(FETCHES):
        fetch(i, i).start()
    def part(i, counts):
        slot = lax.rem(i, FETCHES)
        r = lax.div(i, NNZB // FETCH)
        counts = list(counts)
        fetch(i, slot).wait()
        for n in range(FETCH):
            e = i * FETCH + n
            hi, mid, lo = pieces(buf_ref[slot, n])
            hs_ref[e, 0:BS, :] = hi
            hs_ref[e, BS : 2 * BS, :] = mid
            hs_ref[e, 2 * BS : 3 * BS, :] = lo
            col = cols_ref[r, e - r * NNZB]
            kind = jnp.where(col < RB, 0, 1 + lax.shift_right_logical(col - RB, 3))
            v = col + info_ref[4 + kind]
            code = r * 65536 + e * 64 + v
            source = lax.shift_right_logical(v, 3)
            mine = [source < 3, source == 3, source == 4, source == 5]
            at = jnp.where(mine[0], counts[0], jnp.where(mine[1], counts[1], jnp.where(mine[2], counts[2], counts[3])))
            list_ref[jnp.maximum(source - 2, 0), at] = code
            list_ref[A_B_D, counts[4]] = code
            for p, yes in enumerate((*mine, source >= 3)):
                counts[p] = counts[p] + yes.astype(jnp.int32)

        @pl.when(i + FETCHES < NE // FETCH)
        def _():
            fetch(i + FETCHES, slot).start()

        last = ((i + 1) * FETCH == (r + 1) * NNZB).astype(jnp.int32)
        for p in range(LISTS):
            list_ref[p, counts[p]] = r * 65536 + VZERO
            counts[p] = counts[p] + (counts[p] & last)
        return tuple(counts)

    counts = lax.fori_loop(0, NE // FETCH, part, (jnp.int32(0),) * LISTS)
    for p in range(LISTS):
        cnt_ref[p] = counts[p]
        for i in range(2 * GROUP):
            list_ref[p, counts[p] + i] = VZERO


TABLE = [pltpu.VMEM((VZERO + 1, BS, 2 * W), BF16), pltpu.VMEM((VZERO + 1, BS, W), BF16)]


def convert(hblocks, local_cols, info):
    return pl.pallas_call(
        convert_kernel,
        in_specs=[SM, SM, ANY],
        out_specs=[VM, SM, SM],
        out_shape=[
            pltpu.VMEM((NE, SPLIT * BS, BS), BF16),
            jax.ShapeDtypeStruct((LISTS, MAXE), jnp.int32),
            jax.ShapeDtypeStruct((LISTS,), jnp.int32),
        ],
        scratch_shapes=[pltpu.VMEM((FETCHES, FETCH, BS, BS), F32), pltpu.SemaphoreType.DMA((FETCHES,))],
        compiler_params=pltpu.CompilerParams(vmem_limit_bytes=VMEM_LIMIT),
        cost_estimate=pl.CostEstimate(flops=NE * 4 * BS**3, bytes_accessed=NE * BS * BS * 4, transcendentals=0),
        name="convert",
    )(local_cols, info, hblocks.reshape(NE, BS, BS))


def fill_packs(info_ref, lists_ref, blocks_ref, outs):
    for t in range(4):
        for g in range(GHOST):
            outs[t][g] = blocks_ref[lists_ref[info_ref[t], g]]


PACKS = [pltpu.VMEM((GHOST, BS, W), F32)] * 4


def pack_kernel(info_ref, lists_ref, v_ref, held_ref, *rest):
    outs, sem_ref = rest[:4], rest[4]
    copies = []
    for i in range(RB // 2):
        part = pl.ds(2 * i, 2)
        copies.append(pltpu.make_async_copy(v_ref.at[part], held_ref.at[part], sem_ref.at[i]))
        copies[-1].start()
    for copy in copies:
        copy.wait()
    fill_packs(info_ref, lists_ref, held_ref, outs)


def pack(info, mine, v):
    return pl.pallas_call(
        pack_kernel,
        in_specs=[SM, SM, pl.BlockSpec(memory_space=pltpu.HBM)],
        out_specs=[VM] * 5,
        out_shape=[pltpu.VMEM((RB, BS, W), F32)] + PACKS,
        scratch_shapes=[pltpu.SemaphoreType.DMA((RB // 2,))],
        compiler_params=pltpu.CompilerParams(vmem_limit_bytes=VMEM_LIMIT),
        name="pack",
    )(info, mine, pltpu.with_memory_space_constraint(v, pltpu.HBM))


def add_list(which, group, places, bufs, list_ref, cnt_ref, hs_ref, v12_ref, v3_ref, acc_ref):
    load_zero(v12_ref, v3_ref)
    for place, buf in zip(places, bufs):
        for i in range(buf.shape[0]):
            load_table(v12_ref, v3_ref, place + i, buf[i])
    products(which, group, list_ref, cnt_ref, hs_ref, v12_ref, v3_ref, acc_ref)


def phase_kernel(which, group, places, fresh, list_ref, cnt_ref, hs_ref, *refs):
    bufs = refs[: len(places)]
    acc_ref, v12_ref, v3_ref = refs[-3:]
    if fresh:
        acc_ref[...] = jnp.zeros_like(acc_ref)
    add_list(which, group, places, bufs, list_ref, cnt_ref, hs_ref, v12_ref, v3_ref, acc_ref)


def run_phase(which, group, places, lists, cnt, hs, bufs, acc=None):
    args = [lists, cnt] + [on_chip(x) for x in (hs, *bufs)] + ([] if acc is None else [on_chip(acc)])
    return pl.pallas_call(
        functools.partial(phase_kernel, which, group, places, acc is None),
        in_specs=[SM, SM] + [VM] * (len(args) - 2),
        out_specs=VM,
        out_shape=pltpu.VMEM((RB, BS, W), F32),
        scratch_shapes=TABLE,
        input_output_aliases={} if acc is None else {len(args) - 1: 0},
        compiler_params=pltpu.CompilerParams(vmem_limit_bytes=VMEM_LIMIT),
        cost_estimate=pl.CostEstimate(
            flops=len(places) * NE * 2 * BS**3, bytes_accessed=4 * 2**20, transcendentals=0
        ),
        name=f"phase_{which}",
    )(*args)


def finish_one_kernel(
    list_ref, cnt_ref, info_ref, mine_ref, hs_ref, a_ref, b_ref, d_ref, v_ref, acc_in, first_ref, *rest
):
    outs, tables = rest[:4], rest[4:]
    for r in range(RB):
        first_ref[r] = first_ref[r] - 0.5 * v_ref[r]
    places, bufs = (AT_A, AT_B, AT_D), (a_ref, b_ref, d_ref)
    add_list(A_B_D, 2 * GROUP, places, bufs, list_ref, cnt_ref, hs_ref, *tables, first_ref)
    fill_packs(info_ref, mine_ref, first_ref, outs)


def finish_one(lists, cnt, info, mine, hs, bufs, v, acc):
    return pl.pallas_call(
        finish_one_kernel,
        in_specs=[SM] * 4 + [VM] * 6,
        out_specs=[VM] * 5,
        out_shape=[pltpu.VMEM((RB, BS, W), F32)] + PACKS,
        scratch_shapes=TABLE,
        input_output_aliases={9: 0},
        compiler_params=pltpu.CompilerParams(vmem_limit_bytes=VMEM_LIMIT),
        cost_estimate=pl.CostEstimate(flops=NE * 6 * BS**3, bytes_accessed=8 * 2**20, transcendentals=0),
        name="finish_one",
    )(lists, cnt, info, mine, on_chip(hs), *[on_chip(x) for x in bufs], on_chip(v), on_chip(acc))


def two_sum(a, b):
    s = a + b
    t = s - a
    return s, (a - (s - t)) + (b - t)


def pair_add(ah, al, bh, bl):
    s, e = two_sum(ah, bh)
    e = e + (al + bl)
    h = s + e
    return h, e - (h - s)


def power_scale(biggest):
    q = jnp.full_like(biggest, 2.0**-100)
    qi = jnp.full_like(biggest, 2.0**100)
    for e in (64, 64, 32, 16, 8, 4, 2, 1):
        t = q * (2.0**e)
        up = t <= biggest
        q = jnp.where(up, t, q)
        qi = jnp.where(up, qi * (2.0**-e), qi)
    return q * 2.0, qi * 0.5


def digits(x, bits, count):
    out = []
    x = x * (2.0 ** (bits - 1))
    for i in range(count):
        d = jnp.round(x)
        out.append(d.astype(BF16))
        x = (x - d) * (2.0**bits)
    return out


def gram_of_digits(cols, bits):
    count = len(cols)
    stacked = jnp.concatenate(cols, axis=1)
    full = lax.dot_general(stacked, stacked, (((0,), (0,)), ((), ())), preferred_element_type=F32)
    terms = []
    for w in range(2, 2 * count):
        total = None
        for i in range(1, count + 1):
            j = w - i
            if 1 <= j <= count:
                block = full[(i - 1) * W : i * W, (j - 1) * W : j * W]
                total = block if total is None else total + block
        terms.append(total * (2.0 ** (2 - bits * w)))
    return terms


def lanes_of(rows):
    return lax.broadcasted_iota(jnp.int32, (rows, W), 1)


def pack_symmetric(g):
    lane = lanes_of(BAND)
    small = lanes_of(8)

    def tail(at):
        out = jnp.zeros((8, W), F32)
        for q in range(4):
            moved = pltpu.roll(g[at + 8 * q : at + 8 * q + 8], (BAND * q - at) % W, 1)
            out = jnp.where(lax.shift_right_logical(small, 5) == q, moved, out)
        return out

    zero = jnp.where(lane < 3 * BAND, g[0:BAND], g[2 * BAND : 3 * BAND])
    one = jnp.where(lane >= BAND, g[BAND : 2 * BAND], g[3 * BAND :])
    return jnp.concatenate([zero, tail(2 * BAND)], axis=0), jnp.concatenate([one, tail(3 * BAND)], axis=0)


def unpack_symmetric(zero, one):
    lane = lanes_of(BAND)

    def tail(packed, at):
        return jnp.concatenate([pltpu.roll(packed[BAND:], (at - BAND * q) % W, 1) for q in range(4)], axis=0)

    two = jnp.where(lane >= 3 * BAND, zero[0:BAND], tail(zero, 2 * BAND))
    three = jnp.where(lane < BAND, one[0:BAND], tail(one, 3 * BAND))
    half = jnp.concatenate([zero[0:BAND], one[0:BAND], two, three], axis=0)
    i = lax.shift_right_logical(lax.broadcasted_iota(jnp.int32, (W, W), 0), 5)
    j = lax.shift_right_logical(lax.broadcasted_iota(jnp.int32, (W, W), 1), 5)
    ahead = (j - i) & 3
    return jnp.where((ahead < 2) | ((ahead == 2) & (i < 2)), half, half.T)


def finish_two_kernel(
    list_ref, cnt_ref, info_ref, hs_ref, buf_ref, first_ref, v_ref, acc_in,
    out_ref, keep_ref, send_ref, v12_ref, v3_ref,
):
    add_list(3, GROUP, (AT_D,), (buf_ref,), list_ref, cnt_ref, hs_ref, v12_ref, v3_ref, out_ref)
    biggest = jnp.zeros((BS, W), F32)
    for r in range(RB):
        second = 2.0 * (out_ref[r] - 0.5 * first_ref[r]) - v_ref[r]
        out_ref[r] = second
        biggest = jnp.maximum(biggest, jnp.abs(second))
    biggest = jnp.max(biggest, axis=0, keepdims=True)
    scale, inverse = power_scale(jnp.broadcast_to(biggest, (8, W)))
    scaled = out_ref[...].reshape(RB * BS, W) * inverse[0:1]
    terms = gram_of_digits(digits(scaled, 7, 4), 7)
    hi = terms[0]
    lo = jnp.zeros_like(hi)
    for t in terms[1:]:
        hi, e = two_sum(hi, t)
        lo = lo + e
    wide = jnp.broadcast_to(scale[0:1], (W, W))
    both = wide.T
    core = info_ref[9]
    for i, part in enumerate((hi, lo)):
        zero, one = pack_symmetric((part * wide) * both)
        keep_ref[i] = jnp.where(core == 0, zero, one)
        send_ref[i] = jnp.where(core == 0, one, zero)


def finish_two(lists, cnt, info, hs, buf, first, v, acc):
    return pl.pallas_call(
        finish_two_kernel,
        in_specs=[SM] * 3 + [VM] * 5,
        out_specs=[VM] * 3,
        out_shape=[pltpu.VMEM((RB, BS, W), F32)] + [pltpu.VMEM((2, PACKED, W), F32)] * 2,
        scratch_shapes=TABLE,
        input_output_aliases={7: 0},
        compiler_params=pltpu.CompilerParams(vmem_limit_bytes=VMEM_LIMIT),
        cost_estimate=pl.CostEstimate(flops=NE * 2 * BS**3, bytes_accessed=8 * 2**20, transcendentals=0),
        name="finish_two",
    )(lists, cnt, info, on_chip(hs), on_chip(buf), on_chip(first), on_chip(v), on_chip(acc))


def eliminate(G):
    ri = lax.broadcasted_iota(jnp.int32, (8, W), 0)
    ci = lax.broadcasted_iota(jnp.int32, (8, W), 1)
    nb = W // 8
    A = [G[8 * b : 8 * b + 8, :] for b in range(nb)]
    B = [(ci == ri + 8 * b).astype(F32) for b in range(nb)]
    upper, lower_inv = [], []
    for k in range(nb):
        lanes = [jnp.broadcast_to(A[k][:, 8 * k + c : 8 * k + c + 1], (8, W)) for c in range(8)]
        d = [[jnp.broadcast_to(lanes[c][m : m + 1, :], (8, W)) for c in range(m + 1)] for m in range(8)]
        ra = [jnp.broadcast_to(A[k][m : m + 1, :], (8, W)) for m in range(8)]
        rb = [jnp.broadcast_to(B[k][m : m + 1, :], (8, W)) for m in range(8)]
        cols = {b: [jnp.broadcast_to(A[b][:, 8 * k + c : 8 * k + c + 1], (8, W)) for c in range(8)] for b in range(k + 1, nb)}
        inv = [None] * 8
        l = [[None] * 8 for _ in range(8)]
        for i in range(8):
            inv[i] = 1.0 / d[i][i]
            for m in range(i + 1, 8):
                l[m][i] = d[m][i] * inv[i]
                for c in range(i + 1, m + 1):
                    d[m][c] = d[m][c] - l[m][i] * d[c][i]
            for m in range(i + 1, 8):
                ra[m] = ra[m] - l[m][i] * ra[i]
                rb[m] = rb[m] - l[m][i] * rb[i]
        sa = [ra[i] * inv[i] for i in range(8)]
        sb = [rb[i] * inv[i] for i in range(8)]
        for b in range(k + 1, nb):
            c = cols[b]
            for i in range(8):
                for j in range(i):
                    c[i] = c[i] - l[i][j] * c[j]
                A[b] = A[b] - c[i] * sa[i]
                B[b] = B[b] - c[i] * sb[i]
        pa, pb, pd = ra[0], rb[0], d[0][0]
        for m in range(1, 8):
            pa = jnp.where(ri == m, ra[m], pa)
            pb = jnp.where(ri == m, rb[m], pb)
            pd = jnp.where(ri == m, d[m][m], pd)
        s = 1.0 / jnp.sqrt(pd)
        upper.append(jnp.where(ci >= ri + 8 * k, pa * s, 0.0))
        lower_inv.append(jnp.where(ci <= ri + 8 * k, pb * s, 0.0))
    return jnp.concatenate(upper, axis=0), jnp.concatenate(lower_inv, axis=0)


def dot(a, b, ca, cb):
    return lax.dot_general(a, b, (((ca,), (cb,)), ((), ())), preferred_element_type=F32)


def mm1(a, b, ca=1, cb=0):
    return dot(a.astype(BF16), b.astype(BF16), ca, cb)


def mm3(a, b, ca=1, cb=0):
    ah, al = pieces(a, 2)
    bh, bl = pieces(b, 2)
    return dot(jnp.concatenate([al, ah, ah], axis=ca), jnp.concatenate([bh, bl, bh], axis=cb), ca, cb)


def mm6(a, b, ca=1, cb=0):
    ah, am, al = pieces(a)
    bh, bm, bl = pieces(b)
    return dot(
        jnp.concatenate([al, ah, am, am, ah, ah], axis=ca), jnp.concatenate([bh, bl, bm, bh, bm, bh], axis=cb), ca, cb
    )


def factor_kernel(total, zero_ref, one_ref, inv_ref, factor_ref):
    ri = lax.broadcasted_iota(jnp.int32, (W, W), 0)
    ci = lax.broadcasted_iota(jnp.int32, (W, W), 1)
    eye = (ri == ci).astype(F32)

    def half_lower(x):
        return jnp.where(ri > ci, x, jnp.where(ri == ci, 0.5 * x, 0.0))

    hi, lo = [unpack_symmetric(zero_ref[i], one_ref[i]) * (1.0 / total) for i in range(2)]
    upper, linv = eliminate(hi)

    norm = jnp.sqrt(jnp.sum(hi * eye, axis=0, keepdims=True))
    scale, inverse = power_scale(jnp.broadcast_to(norm, (8, W)))
    wide, wide_inv = jnp.broadcast_to(scale[0:1], (W, W)), jnp.broadcast_to(inverse[0:1], (W, W))
    tall, tall_inv = wide.T, wide_inv.T
    rest = (hi * wide_inv) * tall_inv
    small = (lo * wide_inv) * tall_inv
    for t in gram_of_digits(digits(upper * wide_inv, 8, 4), 8):
        rest, e = two_sum(rest, -t)
        small = small + e
    rest = ((rest + small) * wide) * tall

    off = mm3(mm3(linv, rest), linv, 1, 1)
    defect = eye - mm6(linv, upper, 1, 1)
    close = jnp.sum(off * off) < 1e-5

    @pl.when(close)
    def _():
        x = half_lower(off)
        z = mm1(x, x - defect) + defect
        x = half_lower(off - mm1(x, x, 1, 1))
        inv_ref[...] = linv + mm3(z - x, linv)
        factor_ref[...] = upper + mm3(x, upper, 0, 0)

    @pl.when(jnp.logical_not(close))
    def _():
        u2, l2 = eliminate(eye + off)
        factor = mm6(u2, upper)
        inv = mm6(l2, linv)
        inv_ref[...] = inv + mm6(eye - mm6(inv, factor, 1, 1), inv)
        factor_ref[...] = factor


def factors(zero, one, total):
    return pl.pallas_call(
        functools.partial(factor_kernel, float(total)),
        in_specs=[VM, VM],
        out_specs=[VM, VM],
        out_shape=[pltpu.VMEM((W, W), F32), jax.ShapeDtypeStruct((W, W), F32)],
        compiler_params=pltpu.CompilerParams(vmem_limit_bytes=VMEM_LIMIT),
        name="factors",
    )(on_chip(zero), on_chip(one))


def basis_kernel(s_ref, t_ref, out_ref):
    i = pl.program_id(0)
    out_ref[...] = mm6(s_ref[pl.ds(i * 8, 8)].reshape(8 * BS, W), t_ref[...], 1, 1)


def basis_of(second, inv):
    return pl.pallas_call(
        basis_kernel,
        grid=(RB // 8,),
        in_specs=[VM, VM],
        out_specs=pl.BlockSpec((8 * BS, W), lambda i: (i, 0)),
        out_shape=jax.ShapeDtypeStruct((RB * BS, W), F32),
        compiler_params=pltpu.CompilerParams(vmem_limit_bytes=VMEM_LIMIT),
        name="basis",
    )(on_chip(second), on_chip(inv))


def shards(vectors, hblocks, local_cols, ghost_lists):
    count = lax.axis_size("rows")
    me = lax.axis_index("rows")
    chips = count // 2
    core = me % 2
    odd = (me // 2) % 2

    def to_chip(i, by):
        return ((i // 2 + by) % chips) * 2 + i % 2

    pair_c = [(i, i ^ 1) for i in range(count)]
    pair_a = [(i, to_chip(i, 1 if (i // 2) % 2 == 0 else -1)) for i in range(count)]
    pair_b = [(i, to_chip(i, -1 if (i // 2) % 2 == 0 else 1)) for i in range(count)]
    pair_d = [(i, (i + (1 if i % 2 else -1)) % count) for i in range(count)]

    mine = lax.dynamic_index_in_dim(ghost_lists, me, 0, keepdims=False)
    info = jnp.stack(
        [
            1 + core,
            3 * odd,
            3 - 3 * odd,
            2 - core,
            jnp.zeros_like(me),
            jnp.where(odd == 1, AT_A, AT_B) - 16,
            jnp.where(core == 1, AT_C, AT_D) - 24,
            jnp.where(core == 1, AT_D, AT_C) - 32,
            jnp.where(odd == 1, AT_B, AT_A) - 40,
            core,
        ]
    ).astype(jnp.int32)

    v = vectors.reshape(RB, BS, W)
    move = functools.partial(lax.ppermute, axis_name="rows")

    def exchange(packs):
        return [move(x, perm=perm) for x, perm in zip(packs, (pair_c, pair_a, pair_b, pair_d))]

    v, *packs = pack(info, mine, v)
    c, a, b, d = exchange(packs)
    hs, lists, cnt = convert(hblocks, local_cols, info)
    acc = run_phase(0, 2 * GROUP, (OWN, AT_C), lists, cnt, hs, [v, c])
    first, *packs = finish_one(lists, cnt, info, mine, hs, [a, b, d], v, acc)

    c, a, b, d = exchange(packs)
    acc = run_phase(0, 2 * GROUP, (OWN, AT_C), lists, cnt, hs, [first, c])
    acc = run_phase(1, GROUP, (AT_A,), lists, cnt, hs, [a], acc)
    acc = run_phase(2, GROUP, (AT_B,), lists, cnt, hs, [b], acc)
    second, kept, sent = finish_two(lists, cnt, info, hs, d, first, v, acc)

    theirs = move(sent, perm=pair_c)
    pair = pair_add(kept[0], kept[1], theirs[0], theirs[1])
    for shift in (1, 3, 5):
        mine = jnp.stack(pair)
        one, three, two = [move(mine, perm=[(i, i ^ (by << shift)) for i in range(count)]) for by in (1, 3, 2)]
        pair = pair_add(*pair_add(*pair, one[0], one[1]), *pair_add(two[0], two[1], three[0], three[1]))
    kept = jnp.stack(pair)
    other = move(kept, perm=pair_c)
    first_core = core == 0
    zero, one = jnp.where(first_core, kept, other), jnp.where(first_core, other, kept)
    inv, factor = factors(zero, one, RB * BS * count)
    return basis_of(second, inv), factor


def solution(mesh):
    in_specs = (P("rows", None), P("rows", None, None, None), P("rows", None), P())
    out_specs = (P("rows", None), P())
    return jax.shard_map(shards, mesh=mesh, in_specs=in_specs, out_specs=out_specs, check_vma=False)
```

```python
import functools

import jax
import jax.numpy as jnp
from jax import lax
from jax.experimental import pallas as pl
from jax.experimental.pallas import tpu as pltpu
from jax.sharding import PartitionSpec as P

BS = 128
W = 128
RB = 16
GHOST = 8
NNZB = 20
NE = RB * NNZB
SPLIT = 3
BAND = W // 4
PACKED = BAND + 8
A_B_D = 4
VZERO = 48
MAXE = NE + 48
OWN, AT_C, AT_A, AT_B, AT_D = 0, 16, 24, 32, 40
LISTS = 5
GROUP = 8
FETCH, FETCHES = 10, 8
VMEM_LIMIT = 26 * 1024 * 1024
F32 = jnp.float32
BF16 = jnp.bfloat16
HIGHEST = lax.Precision.HIGHEST

ANY = pl.BlockSpec(memory_space=pl.ANY)
VM = pl.BlockSpec(memory_space=pltpu.VMEM)
SM = pl.BlockSpec(memory_space=pltpu.SMEM)


def on_chip(x):
    return pltpu.with_memory_space_constraint(x, pltpu.VMEM)


def pieces(x, count=SPLIT):
    out = []
    for _ in range(count - 1):
        part = x.astype(BF16)
        out.append(part)
        x = x - part.astype(F32)
    out.append(x.astype(BF16))
    return out


def load_table(v12_ref, v3_ref, at, block):
    hi, mid, lo = pieces(block)
    v12_ref[at, :, 0:W] = hi
    v12_ref[at, :, W : 2 * W] = mid
    v3_ref[at] = lo


def load_zero(v12_ref, v3_ref):
    v12_ref[VZERO] = jnp.zeros((BS, 2 * W), BF16)
    v3_ref[VZERO] = jnp.zeros((BS, W), BF16)


def group_of_products(which, first, count, list_ref, hs_ref, v12_ref, v3_ref, acc_ref):
    for i in range(count):
        one = list_ref[which, first + 2 * i]
        two = list_ref[which, first + 2 * i + 1]
        row = lax.shift_right_logical(one, 16)
        e1 = lax.shift_right_logical(one, 6) & 1023
        e2 = lax.shift_right_logical(two, 6) & 1023
        s1 = one & 63
        s2 = two & 63
        lhs = jnp.concatenate([hs_ref[e1], hs_ref[e2]], axis=1)
        rhs = jnp.concatenate([v12_ref[s1], v12_ref[s2]], axis=0)
        low = jnp.concatenate([v3_ref[s1], v3_ref[s2]], axis=0)
        big = jnp.dot(lhs, rhs, preferred_element_type=F32)
        small = jnp.dot(lhs[0:BS], low, preferred_element_type=F32)
        total = big[0:BS, 0:W] + (
            (big[0:BS, W:] + big[BS : 2 * BS, 0:W]) + (big[BS : 2 * BS, W:] + big[2 * BS :, 0:W] + small)
        )
        acc_ref[row] = acc_ref[row] + total


def products(which, group, list_ref, cnt_ref, *refs):
    def large(g, carry):
        group_of_products(which, g * (2 * group), group, list_ref, *refs)
        return carry

    def small(g, carry):
        group_of_products(which, begin + g * (2 * GROUP), GROUP, list_ref, *refs)
        return carry

    count = cnt_ref[which]
    begin = 0
    if group > GROUP:
        steps = lax.div(count, 2 * group)
        lax.fori_loop(0, steps, large, 0)
        begin = steps * (2 * group)
    lax.fori_loop(0, lax.div(count - begin + (2 * GROUP - 1), 2 * GROUP), small, 0)


def convert_kernel(codes_ref, h_ref, hs_ref, list_ref, cnt_ref, buf_ref, sem_ref):
    def fetch(i, slot):
        return pltpu.make_async_copy(h_ref.at[pl.ds(i * FETCH, FETCH)], buf_ref.at[slot], sem_ref.at[slot])

    for i in range(FETCHES):
        fetch(i, i).start()
    def part(i, counts):
        slot = lax.rem(i, FETCHES)
        r = lax.div(i, NNZB // FETCH)
        counts = list(counts)
        fetch(i, slot).wait()
        for n in range(FETCH):
            e = i * FETCH + n
            hi, mid, lo = pieces(buf_ref[slot, n])
            hs_ref[e, 0:BS, :] = hi
            hs_ref[e, BS : 2 * BS, :] = mid
            hs_ref[e, 2 * BS : 3 * BS, :] = lo
            code = codes_ref[r, e - r * NNZB]
            source = lax.shift_right_logical(code, 3) & 7
            mine = [source < 3, source == 3, source == 4, source == 5]
            at = jnp.where(mine[0], counts[0], jnp.where(mine[1], counts[1], jnp.where(mine[2], counts[2], counts[3])))
            list_ref[jnp.maximum(source - 2, 0), at] = code
            list_ref[A_B_D, counts[4]] = code
            for p, yes in enumerate((*mine, source >= 3)):
                counts[p] = counts[p] + yes.astype(jnp.int32)

        @pl.when(i + FETCHES < NE // FETCH)
        def _():
            fetch(i + FETCHES, slot).start()

        last = ((i + 1) * FETCH == (r + 1) * NNZB).astype(jnp.int32)
        for p in range(LISTS):
            list_ref[p, counts[p]] = r * 65536 + VZERO
            counts[p] = counts[p] + (counts[p] & last)
        return tuple(counts)

    counts = lax.fori_loop(0, NE // FETCH, part, (jnp.int32(0),) * LISTS)
    for p in range(LISTS):
        cnt_ref[p] = counts[p]
        for i in range(2 * GROUP):
            list_ref[p, counts[p] + i] = VZERO


TABLE = [pltpu.VMEM((VZERO + 1, BS, 2 * W), BF16), pltpu.VMEM((VZERO + 1, BS, W), BF16)]


def convert(hblocks, codes):
    return pl.pallas_call(
        convert_kernel,
        in_specs=[SM, ANY],
        out_specs=[VM, SM, SM],
        out_shape=[
            pltpu.VMEM((NE, SPLIT * BS, BS), BF16),
            jax.ShapeDtypeStruct((LISTS, MAXE), jnp.int32),
            jax.ShapeDtypeStruct((LISTS,), jnp.int32),
        ],
        scratch_shapes=[pltpu.VMEM((FETCHES, FETCH, BS, BS), F32), pltpu.SemaphoreType.DMA((FETCHES,))],
        compiler_params=pltpu.CompilerParams(vmem_limit_bytes=VMEM_LIMIT),
        cost_estimate=pl.CostEstimate(flops=NE * 4 * BS**3, bytes_accessed=NE * BS * BS * 4, transcendentals=0),
        name="convert",
    )(codes, hblocks.reshape(NE, BS, BS))


def fill_packs(info_ref, lists_ref, blocks_ref, outs):
    for t in range(4):
        for g in range(GHOST):
            outs[t][g] = blocks_ref[lists_ref[info_ref[t], g]]


PACKS = [pltpu.VMEM((GHOST, BS, W), F32)] * 4


def pack_kernel(info_ref, lists_ref, v_ref, held_ref, *rest):
    outs, sem_ref = rest[:4], rest[4]
    copies = []
    for i in range(RB // 2):
        part = pl.ds(2 * i, 2)
        copies.append(pltpu.make_async_copy(v_ref.at[part], held_ref.at[part], sem_ref.at[i]))
        copies[-1].start()
    for copy in copies:
        copy.wait()
    fill_packs(info_ref, lists_ref, held_ref, outs)


def pack(info, mine, v):
    return pl.pallas_call(
        pack_kernel,
        in_specs=[SM, SM, pl.BlockSpec(memory_space=pltpu.HBM)],
        out_specs=[VM] * 5,
        out_shape=[pltpu.VMEM((RB, BS, W), F32)] + PACKS,
        scratch_shapes=[pltpu.SemaphoreType.DMA((RB // 2,))],
        compiler_params=pltpu.CompilerParams(vmem_limit_bytes=VMEM_LIMIT),
        name="pack",
    )(info, mine, pltpu.with_memory_space_constraint(v, pltpu.HBM))


def add_list(which, group, places, bufs, list_ref, cnt_ref, hs_ref, v12_ref, v3_ref, acc_ref):
    load_zero(v12_ref, v3_ref)
    for place, buf in zip(places, bufs):
        for i in range(buf.shape[0]):
            load_table(v12_ref, v3_ref, place + i, buf[i])
    products(which, group, list_ref, cnt_ref, hs_ref, v12_ref, v3_ref, acc_ref)


def phase_kernel(which, group, places, fresh, list_ref, cnt_ref, hs_ref, *refs):
    bufs = refs[: len(places)]
    acc_ref, v12_ref, v3_ref = refs[-3:]
    if fresh:
        acc_ref[...] = jnp.zeros_like(acc_ref)
    add_list(which, group, places, bufs, list_ref, cnt_ref, hs_ref, v12_ref, v3_ref, acc_ref)


def run_phase(which, group, places, lists, cnt, hs, bufs, acc=None):
    args = [lists, cnt] + [on_chip(x) for x in (hs, *bufs)] + ([] if acc is None else [on_chip(acc)])
    return pl.pallas_call(
        functools.partial(phase_kernel, which, group, places, acc is None),
        in_specs=[SM, SM] + [VM] * (len(args) - 2),
        out_specs=VM,
        out_shape=pltpu.VMEM((RB, BS, W), F32),
        scratch_shapes=TABLE,
        input_output_aliases={} if acc is None else {len(args) - 1: 0},
        compiler_params=pltpu.CompilerParams(vmem_limit_bytes=VMEM_LIMIT),
        cost_estimate=pl.CostEstimate(
            flops=len(places) * NE * 2 * BS**3, bytes_accessed=4 * 2**20, transcendentals=0
        ),
        name=f"phase_{which}",
    )(*args)


def finish_one_kernel(
    list_ref, cnt_ref, info_ref, mine_ref, hs_ref, a_ref, b_ref, d_ref, v_ref, acc_in, first_ref, *rest
):
    outs, tables = rest[:4], rest[4:]
    for r in range(RB):
        first_ref[r] = first_ref[r] - 0.5 * v_ref[r]
    places, bufs = (AT_A, AT_B, AT_D), (a_ref, b_ref, d_ref)
    add_list(A_B_D, 2 * GROUP, places, bufs, list_ref, cnt_ref, hs_ref, *tables, first_ref)
    fill_packs(info_ref, mine_ref, first_ref, outs)


def finish_one(lists, cnt, info, mine, hs, bufs, v, acc):
    return pl.pallas_call(
        finish_one_kernel,
        in_specs=[SM] * 4 + [VM] * 6,
        out_specs=[VM] * 5,
        out_shape=[pltpu.VMEM((RB, BS, W), F32)] + PACKS,
        scratch_shapes=TABLE,
        input_output_aliases={9: 0},
        compiler_params=pltpu.CompilerParams(vmem_limit_bytes=VMEM_LIMIT),
        cost_estimate=pl.CostEstimate(flops=NE * 6 * BS**3, bytes_accessed=8 * 2**20, transcendentals=0),
        name="finish_one",
    )(lists, cnt, info, mine, on_chip(hs), *[on_chip(x) for x in bufs], on_chip(v), on_chip(acc))


def two_sum(a, b):
    s = a + b
    t = s - a
    return s, (a - (s - t)) + (b - t)


def pair_add(ah, al, bh, bl):
    s, e = two_sum(ah, bh)
    e = e + (al + bl)
    h = s + e
    return h, e - (h - s)


def power_scale(biggest):
    q = jnp.full_like(biggest, 2.0**-100)
    qi = jnp.full_like(biggest, 2.0**100)
    for e in (64, 64, 32, 16, 8, 4, 2, 1):
        t = q * (2.0**e)
        up = t <= biggest
        q = jnp.where(up, t, q)
        qi = jnp.where(up, qi * (2.0**-e), qi)
    return q * 2.0, qi * 0.5


def digits(x, bits, count):
    out = []
    x = x * (2.0 ** (bits - 1))
    for i in range(count):
        d = jnp.round(x)
        out.append(d.astype(BF16))
        x = (x - d) * (2.0**bits)
    return out


def gram_of_digits(cols, bits):
    count = len(cols)
    stacked = jnp.concatenate(cols, axis=1)
    full = lax.dot_general(stacked, stacked, (((0,), (0,)), ((), ())), preferred_element_type=F32)
    terms = []
    for w in range(2, 2 * count):
        total = None
        for i in range(1, count + 1):
            j = w - i
            if 1 <= j <= count:
                block = full[(i - 1) * W : i * W, (j - 1) * W : j * W]
                total = block if total is None else total + block
        terms.append(total * (2.0 ** (2 - bits * w)))
    return terms


def lanes_of(rows):
    return lax.broadcasted_iota(jnp.int32, (rows, W), 1)


def pack_symmetric(g):
    lane = lanes_of(BAND)
    small = lanes_of(8)

    def tail(at):
        out = jnp.zeros((8, W), F32)
        for q in range(4):
            moved = pltpu.roll(g[at + 8 * q : at + 8 * q + 8], (BAND * q - at) % W, 1)
            out = jnp.where(lax.shift_right_logical(small, 5) == q, moved, out)
        return out

    zero = jnp.where(lane < 3 * BAND, g[0:BAND], g[2 * BAND : 3 * BAND])
    one = jnp.where(lane >= BAND, g[BAND : 2 * BAND], g[3 * BAND :])
    return jnp.concatenate([zero, tail(2 * BAND)], axis=0), jnp.concatenate([one, tail(3 * BAND)], axis=0)


def unpack_symmetric(zero, one):
    lane = lanes_of(BAND)

    def tail(packed, at):
        return jnp.concatenate([pltpu.roll(packed[BAND:], (at - BAND * q) % W, 1) for q in range(4)], axis=0)

    two = jnp.where(lane >= 3 * BAND, zero[0:BAND], tail(zero, 2 * BAND))
    three = jnp.where(lane < BAND, one[0:BAND], tail(one, 3 * BAND))
    half = jnp.concatenate([zero[0:BAND], one[0:BAND], two, three], axis=0)
    i = lax.shift_right_logical(lax.broadcasted_iota(jnp.int32, (W, W), 0), 5)
    j = lax.shift_right_logical(lax.broadcasted_iota(jnp.int32, (W, W), 1), 5)
    ahead = (j - i) & 3
    return jnp.where((ahead < 2) | ((ahead == 2) & (i < 2)), half, half.T)


def finish_two_kernel(
    list_ref, cnt_ref, info_ref, hs_ref, buf_ref, first_ref, v_ref, acc_in,
    out_ref, keep_ref, send_ref, v12_ref, v3_ref,
):
    add_list(3, GROUP, (AT_D,), (buf_ref,), list_ref, cnt_ref, hs_ref, v12_ref, v3_ref, out_ref)
    biggest = jnp.zeros((BS, W), F32)
    for r in range(RB):
        second = 2.0 * (out_ref[r] - 0.5 * first_ref[r]) - v_ref[r]
        out_ref[r] = second
        biggest = jnp.maximum(biggest, jnp.abs(second))
    biggest = jnp.max(biggest, axis=0, keepdims=True)
    scale, inverse = power_scale(jnp.broadcast_to(biggest, (8, W)))
    scaled = out_ref[...].reshape(RB * BS, W) * inverse[0:1]
    terms = gram_of_digits(digits(scaled, 7, 4), 7)
    hi = terms[0]
    lo = jnp.zeros_like(hi)
    for t in terms[1:]:
        hi, e = two_sum(hi, t)
        lo = lo + e
    wide = jnp.broadcast_to(scale[0:1], (W, W))
    both = wide.T
    core = info_ref[4]
    for i, part in enumerate((hi, lo)):
        zero, one = pack_symmetric((part * wide) * both)
        keep_ref[i] = jnp.where(core == 0, zero, one)
        send_ref[i] = jnp.where(core == 0, one, zero)


def finish_two(lists, cnt, info, hs, buf, first, v, acc):
    return pl.pallas_call(
        finish_two_kernel,
        in_specs=[SM] * 3 + [VM] * 5,
        out_specs=[VM] * 3,
        out_shape=[pltpu.VMEM((RB, BS, W), F32)] + [pltpu.VMEM((2, PACKED, W), F32)] * 2,
        scratch_shapes=TABLE,
        input_output_aliases={7: 0},
        compiler_params=pltpu.CompilerParams(vmem_limit_bytes=VMEM_LIMIT),
        cost_estimate=pl.CostEstimate(flops=NE * 2 * BS**3, bytes_accessed=8 * 2**20, transcendentals=0),
        name="finish_two",
    )(lists, cnt, info, on_chip(hs), on_chip(buf), on_chip(first), on_chip(v), on_chip(acc))


def eliminate(G):
    ri = lax.broadcasted_iota(jnp.int32, (8, W), 0)
    ci = lax.broadcasted_iota(jnp.int32, (8, W), 1)
    nb = W // 8
    A = [G[8 * b : 8 * b + 8, :] for b in range(nb)]
    B = [(ci == ri + 8 * b).astype(F32) for b in range(nb)]
    upper, lower_inv = [], []
    for k in range(nb):
        lanes = [jnp.broadcast_to(A[k][:, 8 * k + c : 8 * k + c + 1], (8, W)) for c in range(8)]
        d = [[jnp.broadcast_to(lanes[c][m : m + 1, :], (8, W)) for c in range(m + 1)] for m in range(8)]
        ra = [jnp.broadcast_to(A[k][m : m + 1, :], (8, W)) for m in range(8)]
        rb = [jnp.broadcast_to(B[k][m : m + 1, :], (8, W)) for m in range(8)]
        cols = {b: [jnp.broadcast_to(A[b][:, 8 * k + c : 8 * k + c + 1], (8, W)) for c in range(8)] for b in range(k + 1, nb)}
        inv = [None] * 8
        l = [[None] * 8 for _ in range(8)]
        for i in range(8):
            inv[i] = 1.0 / d[i][i]
            for m in range(i + 1, 8):
                l[m][i] = d[m][i] * inv[i]
                for c in range(i + 1, m + 1):
                    d[m][c] = d[m][c] - l[m][i] * d[c][i]
            for m in range(i + 1, 8):
                ra[m] = ra[m] - l[m][i] * ra[i]
                rb[m] = rb[m] - l[m][i] * rb[i]
        sa = [ra[i] * inv[i] for i in range(8)]
        sb = [rb[i] * inv[i] for i in range(8)]
        for b in range(k + 1, nb):
            c = cols[b]
            for i in range(8):
                for j in range(i):
                    c[i] = c[i] - l[i][j] * c[j]
                A[b] = A[b] - c[i] * sa[i]
                B[b] = B[b] - c[i] * sb[i]
        pa, pb, pd = ra[0], rb[0], d[0][0]
        for m in range(1, 8):
            pa = jnp.where(ri == m, ra[m], pa)
            pb = jnp.where(ri == m, rb[m], pb)
            pd = jnp.where(ri == m, d[m][m], pd)
        s = 1.0 / jnp.sqrt(pd)
        upper.append(jnp.where(ci >= ri + 8 * k, pa * s, 0.0))
        lower_inv.append(jnp.where(ci <= ri + 8 * k, pb * s, 0.0))
    return jnp.concatenate(upper, axis=0), jnp.concatenate(lower_inv, axis=0)


def dot(a, b, ca, cb):
    return lax.dot_general(a, b, (((ca,), (cb,)), ((), ())), preferred_element_type=F32)


def mm1(a, b, ca=1, cb=0):
    return dot(a.astype(BF16), b.astype(BF16), ca, cb)


def mm3(a, b, ca=1, cb=0):
    ah, al = pieces(a, 2)
    bh, bl = pieces(b, 2)
    return dot(jnp.concatenate([al, ah, ah], axis=ca), jnp.concatenate([bh, bl, bh], axis=cb), ca, cb)


def mm6(a, b, ca=1, cb=0):
    ah, am, al = pieces(a)
    bh, bm, bl = pieces(b)
    return dot(
        jnp.concatenate([al, ah, am, am, ah, ah], axis=ca), jnp.concatenate([bh, bl, bm, bh, bm, bh], axis=cb), ca, cb
    )


def factor_kernel(total, zero_ref, one_ref, inv_ref, factor_ref):
    ri = lax.broadcasted_iota(jnp.int32, (W, W), 0)
    ci = lax.broadcasted_iota(jnp.int32, (W, W), 1)
    eye = (ri == ci).astype(F32)

    def half_lower(x):
        return jnp.where(ri > ci, x, jnp.where(ri == ci, 0.5 * x, 0.0))

    hi, lo = [unpack_symmetric(zero_ref[i], one_ref[i]) * (1.0 / total) for i in range(2)]
    upper, linv = eliminate(hi)

    norm = jnp.sqrt(jnp.sum(hi * eye, axis=0, keepdims=True))
    scale, inverse = power_scale(jnp.broadcast_to(norm, (8, W)))
    wide, wide_inv = jnp.broadcast_to(scale[0:1], (W, W)), jnp.broadcast_to(inverse[0:1], (W, W))
    tall, tall_inv = wide.T, wide_inv.T
    rest = (hi * wide_inv) * tall_inv
    small = (lo * wide_inv) * tall_inv
    for t in gram_of_digits(digits(upper * wide_inv, 8, 4), 8):
        rest, e = two_sum(rest, -t)
        small = small + e
    rest = ((rest + small) * wide) * tall

    off = mm3(mm3(linv, rest), linv, 1, 1)
    defect = eye - mm6(linv, upper, 1, 1)
    close = jnp.sum(off * off) < 1e-5

    @pl.when(close)
    def _():
        x = half_lower(off)
        z = mm1(x, x - defect) + defect
        x = half_lower(off - mm1(x, x, 1, 1))
        inv_ref[...] = linv + mm3(z - x, linv)
        factor_ref[...] = upper + mm3(x, upper, 0, 0)

    @pl.when(jnp.logical_not(close))
    def _():
        u2, l2 = eliminate(eye + off)
        factor = mm6(u2, upper)
        inv = mm6(l2, linv)
        inv_ref[...] = inv + mm6(eye - mm6(inv, factor, 1, 1), inv)
        factor_ref[...] = factor


def factors(zero, one, total):
    return pl.pallas_call(
        functools.partial(factor_kernel, float(total)),
        in_specs=[VM, VM],
        out_specs=[VM, VM],
        out_shape=[pltpu.VMEM((W, W), F32), jax.ShapeDtypeStruct((W, W), F32)],
        compiler_params=pltpu.CompilerParams(vmem_limit_bytes=VMEM_LIMIT),
        name="factors",
    )(on_chip(zero), on_chip(one))


def basis_kernel(s_ref, t_ref, out_ref):
    i = pl.program_id(0)
    out_ref[...] = mm6(s_ref[pl.ds(i * 8, 8)].reshape(8 * BS, W), t_ref[...], 1, 1)


def basis_of(second, inv):
    return pl.pallas_call(
        basis_kernel,
        grid=(RB // 8,),
        in_specs=[VM, VM],
        out_specs=pl.BlockSpec((8 * BS, W), lambda i: (i, 0)),
        out_shape=jax.ShapeDtypeStruct((RB * BS, W), F32),
        compiler_params=pltpu.CompilerParams(vmem_limit_bytes=VMEM_LIMIT),
        name="basis",
    )(on_chip(second), on_chip(inv))


def shards(vectors, hblocks, local_cols, ghost_lists):
    count = lax.axis_size("rows")
    me = lax.axis_index("rows")
    chips = count // 2
    core = me % 2
    odd = (me // 2) % 2

    def to_chip(i, by):
        return ((i // 2 + by) % chips) * 2 + i % 2

    pair_c = [(i, i ^ 1) for i in range(count)]
    pair_a = [(i, to_chip(i, 1 if (i // 2) % 2 == 0 else -1)) for i in range(count)]
    pair_b = [(i, to_chip(i, -1 if (i // 2) % 2 == 0 else 1)) for i in range(count)]
    pair_d = [(i, (i + (1 if i % 2 else -1)) % count) for i in range(count)]

    mine = lax.dynamic_index_in_dim(ghost_lists, me, 0, keepdims=False)
    info = jnp.stack([1 + core, 3 * odd, 3 - 3 * odd, 2 - core, core]).astype(jnp.int32)
    moved = [
        jnp.where(odd == 1, AT_A, AT_B),
        jnp.where(core == 1, AT_C, AT_D),
        jnp.where(core == 1, AT_D, AT_C),
        jnp.where(odd == 1, AT_B, AT_A),
    ]
    at = local_cols
    for k in range(4):
        begin = RB + k * GHOST
        inside = (local_cols >= begin) & (local_cols < begin + GHOST)
        at = jnp.where(inside, local_cols - begin + moved[k], at)
    row = lax.broadcasted_iota(jnp.int32, (RB, NNZB), 0)
    entry = row * NNZB + lax.broadcasted_iota(jnp.int32, (RB, NNZB), 1)
    codes = (row * 65536 + entry * 64 + at).astype(jnp.int32)

    v = vectors.reshape(RB, BS, W)
    move = functools.partial(lax.ppermute, axis_name="rows")

    v, *packs = pack(info, mine, v)
    c, a, b = [move(x, perm=perm) for x, perm in zip(packs, (pair_c, pair_a, pair_b))]
    hs, lists, cnt = convert(hblocks, codes)
    late, lists = lax.optimization_barrier((packs[3], lists))
    d = move(late, perm=pair_d)
    acc = run_phase(0, 2 * GROUP, (OWN, AT_C), lists, cnt, hs, [v, c])
    first, *packs = finish_one(lists, cnt, info, mine, hs, [a, b, d], v, acc)

    c, a, b = [move(x, perm=perm) for x, perm in zip(packs, (pair_c, pair_a, pair_b))]
    acc = run_phase(0, 2 * GROUP, (OWN, AT_C), lists, cnt, hs, [first, c])
    late, acc = lax.optimization_barrier((packs[3], acc))
    d = move(late, perm=pair_d)
    acc = run_phase(1, GROUP, (AT_A,), lists, cnt, hs, [a], acc)
    acc = run_phase(2, GROUP, (AT_B,), lists, cnt, hs, [b], acc)
    second, kept, sent = finish_two(lists, cnt, info, hs, d, first, v, acc)

    theirs = move(sent, perm=pair_c)
    pair = pair_add(kept[0], kept[1], theirs[0], theirs[1])
    for shift in (1, 3, 5):
        mine = jnp.stack(pair)
        one, three, two = [move(mine, perm=[(i, i ^ (by << shift)) for i in range(count)]) for by in (1, 3, 2)]
        pair = pair_add(*pair_add(*pair, one[0], one[1]), *pair_add(two[0], two[1], three[0], three[1]))
    kept = jnp.stack(pair)
    other = move(kept, perm=pair_c)
    first_core = core == 0
    zero, one = jnp.where(first_core, kept, other), jnp.where(first_core, other, kept)
    inv, factor = factors(zero, one, RB * BS * count)
    return basis_of(second, inv), factor


def solution(mesh):
    in_specs = (P("rows", None), P("rows", None, None, None), P("rows", None), P())
    out_specs = (P("rows", None), P())
    return jax.shard_map(shards, mesh=mesh, in_specs=in_specs, out_specs=out_specs, check_vma=False)
```

```python
import functools

import jax
import jax.numpy as jnp
from jax import lax
from jax.experimental import pallas as pl
from jax.experimental.pallas import tpu as pltpu
from jax.sharding import PartitionSpec as P

BS = 128
W = 128
RB = 16
GHOST = 8
NNZB = 20
NE = RB * NNZB
SPLIT = 3
BAND = W // 4
PACKED = BAND + 8
A_B_D = 4
VZERO = 48
MAXE = NE + 48
OWN, AT_C, AT_A, AT_B, AT_D = 0, 16, 24, 32, 40
LISTS = 5
GROUP = 8
FETCH, FETCHES = 10, 8
VMEM_LIMIT = 26 * 1024 * 1024
F32 = jnp.float32
BF16 = jnp.bfloat16
HIGHEST = lax.Precision.HIGHEST

ANY = pl.BlockSpec(memory_space=pl.ANY)
VM = pl.BlockSpec(memory_space=pltpu.VMEM)
SM = pl.BlockSpec(memory_space=pltpu.SMEM)


def on_chip(x):
    return pltpu.with_memory_space_constraint(x, pltpu.VMEM)


def pieces(x, count=SPLIT):
    out = []
    for _ in range(count - 1):
        part = x.astype(BF16)
        out.append(part)
        x = x - part.astype(F32)
    out.append(x.astype(BF16))
    return out


def load_table(v12_ref, v3_ref, at, block):
    hi, mid, lo = pieces(block)
    v12_ref[at, :, 0:W] = hi
    v12_ref[at, :, W : 2 * W] = mid
    v3_ref[at] = lo


def load_zero(v12_ref, v3_ref):
    v12_ref[VZERO] = jnp.zeros((BS, 2 * W), BF16)
    v3_ref[VZERO] = jnp.zeros((BS, W), BF16)


def group_of_products(which, first, count, list_ref, hs_ref, v12_ref, v3_ref, acc_ref):
    for i in range(count):
        one = list_ref[which, first + 2 * i]
        two = list_ref[which, first + 2 * i + 1]
        row = lax.shift_right_logical(one, 16)
        e1 = lax.shift_right_logical(one, 6) & 1023
        e2 = lax.shift_right_logical(two, 6) & 1023
        s1 = one & 63
        s2 = two & 63
        lhs = jnp.concatenate([hs_ref[e1], hs_ref[e2]], axis=1)
        rhs = jnp.concatenate([v12_ref[s1], v12_ref[s2]], axis=0)
        low = jnp.concatenate([v3_ref[s1], v3_ref[s2]], axis=0)
        big = jnp.dot(lhs, rhs, preferred_element_type=F32)
        small = jnp.dot(lhs[0:BS], low, preferred_element_type=F32)
        total = big[0:BS, 0:W] + (
            (big[0:BS, W:] + big[BS : 2 * BS, 0:W]) + (big[BS : 2 * BS, W:] + big[2 * BS :, 0:W] + small)
        )
        acc_ref[row] = acc_ref[row] + total


def products(which, group, list_ref, cnt_ref, *refs):
    def large(g, carry):
        group_of_products(which, g * (2 * group), group, list_ref, *refs)
        return carry

    def small(g, carry):
        group_of_products(which, begin + g * (2 * GROUP), GROUP, list_ref, *refs)
        return carry

    count = cnt_ref[which]
    begin = 0
    if group > GROUP:
        steps = lax.div(count, 2 * group)
        lax.fori_loop(0, steps, large, 0)
        begin = steps * (2 * group)
    lax.fori_loop(0, lax.div(count - begin + (2 * GROUP - 1), 2 * GROUP), small, 0)


def convert_kernel(cols_ref, info_ref, h_ref, hs_ref, list_ref, cnt_ref, buf_ref, sem_ref):
    def fetch(i, slot):
        return pltpu.make_async_copy(h_ref.at[pl.ds(i * FETCH, FETCH)], buf_ref.at[slot], sem_ref.at[slot])

    for i in range(FETCHES):
        fetch(i, i).start()
    def part(i, counts):
        slot = lax.rem(i, FETCHES)
        r = lax.div(i, NNZB // FETCH)
        counts = list(counts)
        fetch(i, slot).wait()
        for n in range(FETCH):
            e = i * FETCH + n
            hi, mid, lo = pieces(buf_ref[slot, n])
            hs_ref[e, 0:BS, :] = hi
            hs_ref[e, BS : 2 * BS, :] = mid
            hs_ref[e, 2 * BS : 3 * BS, :] = lo
            col = cols_ref[r, e - r * NNZB]
            kind = jnp.where(col < RB, 0, 1 + lax.shift_right_logical(col - RB, 3))
            v = col + info_ref[4 + kind]
            code = r * 65536 + e * 64 + v
            source = lax.shift_right_logical(v, 3)
            mine = [source < 3, source == 3, source == 4, source == 5]
            at = jnp.where(mine[0], counts[0], jnp.where(mine[1], counts[1], jnp.where(mine[2], counts[2], counts[3])))
            list_ref[jnp.maximum(source - 2, 0), at] = code
            list_ref[A_B_D, counts[4]] = code
            for p, yes in enumerate((*mine, source >= 3)):
                counts[p] = counts[p] + yes.astype(jnp.int32)

        @pl.when(i + FETCHES < NE // FETCH)
        def _():
            fetch(i + FETCHES, slot).start()

        last = ((i + 1) * FETCH == (r + 1) * NNZB).astype(jnp.int32)
        for p in range(LISTS):
            list_ref[p, counts[p]] = r * 65536 + VZERO
            counts[p] = counts[p] + (counts[p] & last)
        return tuple(counts)

    counts = lax.fori_loop(0, NE // FETCH, part, (jnp.int32(0),) * LISTS)
    for p in range(LISTS):
        cnt_ref[p] = counts[p]
        for i in range(2 * GROUP):
            list_ref[p, counts[p] + i] = VZERO


TABLE = [pltpu.VMEM((VZERO + 1, BS, 2 * W), BF16), pltpu.VMEM((VZERO + 1, BS, W), BF16)]


def convert(hblocks, local_cols, info):
    return pl.pallas_call(
        convert_kernel,
        in_specs=[SM, SM, ANY],
        out_specs=[VM, SM, SM],
        out_shape=[
            pltpu.VMEM((NE, SPLIT * BS, BS), BF16),
            jax.ShapeDtypeStruct((LISTS, MAXE), jnp.int32),
            jax.ShapeDtypeStruct((LISTS,), jnp.int32),
        ],
        scratch_shapes=[pltpu.VMEM((FETCHES, FETCH, BS, BS), F32), pltpu.SemaphoreType.DMA((FETCHES,))],
        compiler_params=pltpu.CompilerParams(vmem_limit_bytes=VMEM_LIMIT),
        cost_estimate=pl.CostEstimate(flops=NE * 4 * BS**3, bytes_accessed=NE * BS * BS * 4, transcendentals=0),
        name="convert",
    )(local_cols, info, hblocks.reshape(NE, BS, BS))


def fill_packs(info_ref, lists_ref, blocks_ref, outs):
    def one_of_each(g, carry):
        for t in range(4):
            outs[t][g] = blocks_ref[lists_ref[info_ref[t], g]]
        return carry

    lax.fori_loop(0, GHOST, one_of_each, 0)


PACKS = [pltpu.VMEM((GHOST, BS, W), F32)] * 4


def pack_kernel(info_ref, lists_ref, v_ref, held_ref, *rest):
    outs, sem_ref = rest[:4], rest[4]
    copies = []
    for i in range(RB // 2):
        part = pl.ds(2 * i, 2)
        copies.append(pltpu.make_async_copy(v_ref.at[part], held_ref.at[part], sem_ref.at[i]))
        copies[-1].start()
    for copy in copies:
        copy.wait()
    fill_packs(info_ref, lists_ref, held_ref, outs)


def pack(info, mine, v):
    return pl.pallas_call(
        pack_kernel,
        in_specs=[SM, SM, pl.BlockSpec(memory_space=pltpu.HBM)],
        out_specs=[VM] * 5,
        out_shape=[pltpu.VMEM((RB, BS, W), F32)] + PACKS,
        scratch_shapes=[pltpu.SemaphoreType.DMA((RB // 2,))],
        compiler_params=pltpu.CompilerParams(vmem_limit_bytes=VMEM_LIMIT),
        name="pack",
    )(info, mine, pltpu.with_memory_space_constraint(v, pltpu.HBM))


def add_list(which, group, places, bufs, list_ref, cnt_ref, hs_ref, v12_ref, v3_ref, acc_ref):
    load_zero(v12_ref, v3_ref)
    for place, buf in zip(places, bufs):

        def two(i, carry, place=place, buf=buf):
            load_table(v12_ref, v3_ref, place + 2 * i, buf[2 * i])
            load_table(v12_ref, v3_ref, place + 2 * i + 1, buf[2 * i + 1])
            return carry

        lax.fori_loop(0, buf.shape[0] // 2, two, 0)
    products(which, group, list_ref, cnt_ref, hs_ref, v12_ref, v3_ref, acc_ref)


def phase_kernel(which, group, places, fresh, list_ref, cnt_ref, hs_ref, *refs):
    bufs = refs[: len(places)]
    acc_ref, v12_ref, v3_ref = refs[-3:]
    if fresh:

        def clear(r, carry):
            acc_ref[r] = jnp.zeros((BS, W), F32)
            return carry

        lax.fori_loop(0, RB, clear, 0)
    add_list(which, group, places, bufs, list_ref, cnt_ref, hs_ref, v12_ref, v3_ref, acc_ref)


def run_phase(which, group, places, lists, cnt, hs, bufs, acc=None):
    args = [lists, cnt] + [on_chip(x) for x in (hs, *bufs)] + ([] if acc is None else [on_chip(acc)])
    return pl.pallas_call(
        functools.partial(phase_kernel, which, group, places, acc is None),
        in_specs=[SM, SM] + [VM] * (len(args) - 2),
        out_specs=VM,
        out_shape=pltpu.VMEM((RB, BS, W), F32),
        scratch_shapes=TABLE,
        input_output_aliases={} if acc is None else {len(args) - 1: 0},
        compiler_params=pltpu.CompilerParams(vmem_limit_bytes=VMEM_LIMIT),
        cost_estimate=pl.CostEstimate(
            flops=len(places) * NE * 2 * BS**3, bytes_accessed=4 * 2**20, transcendentals=0
        ),
        name=f"phase_{which}",
    )(*args)


def finish_one_kernel(
    list_ref, cnt_ref, info_ref, mine_ref, hs_ref, a_ref, b_ref, d_ref, v_ref, acc_in, first_ref, *rest
):
    outs, tables = rest[:4], rest[4:]

    def block_row(r, carry):
        first_ref[r] = first_ref[r] - 0.5 * v_ref[r]
        return carry

    lax.fori_loop(0, RB, block_row, 0)
    places, bufs = (AT_A, AT_B, AT_D), (a_ref, b_ref, d_ref)
    add_list(A_B_D, GROUP, places, bufs, list_ref, cnt_ref, hs_ref, *tables, first_ref)
    fill_packs(info_ref, mine_ref, first_ref, outs)


def finish_one(lists, cnt, info, mine, hs, bufs, v, acc):
    return pl.pallas_call(
        finish_one_kernel,
        in_specs=[SM] * 4 + [VM] * 6,
        out_specs=[VM] * 5,
        out_shape=[pltpu.VMEM((RB, BS, W), F32)] + PACKS,
        scratch_shapes=TABLE,
        input_output_aliases={9: 0},
        compiler_params=pltpu.CompilerParams(vmem_limit_bytes=VMEM_LIMIT),
        cost_estimate=pl.CostEstimate(flops=NE * 6 * BS**3, bytes_accessed=8 * 2**20, transcendentals=0),
        name="finish_one",
    )(lists, cnt, info, mine, on_chip(hs), *[on_chip(x) for x in bufs], on_chip(v), on_chip(acc))


def two_sum(a, b):
    s = a + b
    t = s - a
    return s, (a - (s - t)) + (b - t)


def pair_add(ah, al, bh, bl):
    s, e = two_sum(ah, bh)
    e = e + (al + bl)
    h = s + e
    return h, e - (h - s)


def power_scale(biggest):
    q = jnp.full_like(biggest, 2.0**-100)
    qi = jnp.full_like(biggest, 2.0**100)
    for e in (64, 64, 32, 16, 8, 4, 2, 1):
        t = q * (2.0**e)
        up = t <= biggest
        q = jnp.where(up, t, q)
        qi = jnp.where(up, qi * (2.0**-e), qi)
    return q * 2.0, qi * 0.5


def digits(x, bits, count):
    out = []
    x = x * (2.0 ** (bits - 1))
    for i in range(count):
        d = jnp.round(x)
        out.append(d.astype(BF16))
        x = (x - d) * (2.0**bits)
    return out


def gram_of_digits(stacked, count, bits):
    full = lax.dot_general(stacked, stacked, (((0,), (0,)), ((), ())), preferred_element_type=F32)
    terms = []
    for w in range(2, 2 * count):
        total = None
        for i in range(1, count + 1):
            j = w - i
            if 1 <= j <= count:
                block = full[(i - 1) * W : i * W, (j - 1) * W : j * W]
                total = block if total is None else total + block
        terms.append(total * (2.0 ** (2 - bits * w)))
    return terms


def lanes_of(rows):
    return lax.broadcasted_iota(jnp.int32, (rows, W), 1)


def pack_symmetric(g):
    lane = lanes_of(BAND)
    small = lanes_of(8)

    def tail(at):
        out = jnp.zeros((8, W), F32)
        for q in range(4):
            moved = pltpu.roll(g[at + 8 * q : at + 8 * q + 8], (BAND * q - at) % W, 1)
            out = jnp.where(lax.shift_right_logical(small, 5) == q, moved, out)
        return out

    zero = jnp.where(lane < 3 * BAND, g[0:BAND], g[2 * BAND : 3 * BAND])
    one = jnp.where(lane >= BAND, g[BAND : 2 * BAND], g[3 * BAND :])
    return jnp.concatenate([zero, tail(2 * BAND)], axis=0), jnp.concatenate([one, tail(3 * BAND)], axis=0)


def unpack_symmetric(zero, one):
    lane = lanes_of(BAND)

    def tail(packed, at):
        return jnp.concatenate([pltpu.roll(packed[BAND:], (at - BAND * q) % W, 1) for q in range(4)], axis=0)

    two = jnp.where(lane >= 3 * BAND, zero[0:BAND], tail(zero, 2 * BAND))
    three = jnp.where(lane < BAND, one[0:BAND], tail(one, 3 * BAND))
    half = jnp.concatenate([zero[0:BAND], one[0:BAND], two, three], axis=0)
    i = lax.shift_right_logical(lax.broadcasted_iota(jnp.int32, (W, W), 0), 5)
    j = lax.shift_right_logical(lax.broadcasted_iota(jnp.int32, (W, W), 1), 5)
    ahead = (j - i) & 3
    return jnp.where((ahead < 2) | ((ahead == 2) & (i < 2)), half, half.T)


def finish_two_kernel(
    list_ref, cnt_ref, info_ref, hs_ref, buf_ref, first_ref, v_ref, acc_in,
    out_ref, keep_ref, send_ref, v12_ref, v3_ref, digits_ref,
):
    add_list(3, GROUP, (AT_D,), (buf_ref,), list_ref, cnt_ref, hs_ref, v12_ref, v3_ref, out_ref)

    def block_row(r, biggest):
        second = 2.0 * (out_ref[r] - 0.5 * first_ref[r]) - v_ref[r]
        out_ref[r] = second
        return jnp.maximum(biggest, jnp.max(jnp.abs(second).reshape(BS // 8, 8, W), axis=0))

    biggest = lax.fori_loop(0, RB, block_row, jnp.zeros((8, W), F32))
    biggest = jnp.max(biggest, axis=0, keepdims=True)
    scale, inverse = power_scale(jnp.broadcast_to(biggest, (8, W)))

    def block_digits(r, carry):
        for i, d in enumerate(digits(out_ref[r] * inverse[0:1], 7, 4)):
            digits_ref[pl.ds(pl.multiple_of(r * BS, BS), BS), i * W : (i + 1) * W] = d
        return carry

    lax.fori_loop(0, RB, block_digits, 0)
    terms = gram_of_digits(digits_ref[...], 4, 7)
    hi = terms[0]
    lo = jnp.zeros_like(hi)
    for t in terms[1:]:
        hi, e = two_sum(hi, t)
        lo = lo + e
    wide = jnp.broadcast_to(scale[0:1], (W, W))
    both = wide.T
    core = info_ref[9]
    for i, part in enumerate((hi, lo)):
        zero, one = pack_symmetric((part * wide) * both)
        keep_ref[i] = jnp.where(core == 0, zero, one)
        send_ref[i] = jnp.where(core == 0, one, zero)


def finish_two(lists, cnt, info, hs, buf, first, v, acc):
    return pl.pallas_call(
        finish_two_kernel,
        in_specs=[SM] * 3 + [VM] * 5,
        out_specs=[VM] * 3,
        out_shape=[pltpu.VMEM((RB, BS, W), F32)] + [pltpu.VMEM((2, PACKED, W), F32)] * 2,
        scratch_shapes=TABLE + [pltpu.VMEM((RB * BS, 4 * W), BF16)],
        input_output_aliases={7: 0},
        compiler_params=pltpu.CompilerParams(vmem_limit_bytes=VMEM_LIMIT),
        cost_estimate=pl.CostEstimate(flops=NE * 2 * BS**3, bytes_accessed=8 * 2**20, transcendentals=0),
        name="finish_two",
    )(lists, cnt, info, on_chip(hs), on_chip(buf), on_chip(first), on_chip(v), on_chip(acc))


def eliminate(G):
    ri = lax.broadcasted_iota(jnp.int32, (8, W), 0)
    ci = lax.broadcasted_iota(jnp.int32, (8, W), 1)
    nb = W // 8
    A = [G[8 * b : 8 * b + 8, :] for b in range(nb)]
    B = [(ci == ri + 8 * b).astype(F32) for b in range(nb)]
    upper, lower_inv = [], []
    for k in range(nb):
        lanes = [jnp.broadcast_to(A[k][:, 8 * k + c : 8 * k + c + 1], (8, W)) for c in range(8)]
        d = [[jnp.broadcast_to(lanes[c][m : m + 1, :], (8, W)) for c in range(m + 1)] for m in range(8)]
        ra = [jnp.broadcast_to(A[k][m : m + 1, :], (8, W)) for m in range(8)]
        rb = [jnp.broadcast_to(B[k][m : m + 1, :], (8, W)) for m in range(8)]
        cols = {b: [jnp.broadcast_to(A[b][:, 8 * k + c : 8 * k + c + 1], (8, W)) for c in range(8)] for b in range(k + 1, nb)}
        inv = [None] * 8
        l = [[None] * 8 for _ in range(8)]
        for i in range(8):
            inv[i] = 1.0 / d[i][i]
            for m in range(i + 1, 8):
                l[m][i] = d[m][i] * inv[i]
                for c in range(i + 1, m + 1):
                    d[m][c] = d[m][c] - l[m][i] * d[c][i]
            for m in range(i + 1, 8):
                ra[m] = ra[m] - l[m][i] * ra[i]
                rb[m] = rb[m] - l[m][i] * rb[i]
        sa = [ra[i] * inv[i] for i in range(8)]
        sb = [rb[i] * inv[i] for i in range(8)]
        for b in range(k + 1, nb):
            c = cols[b]
            for i in range(8):
                for j in range(i):
                    c[i] = c[i] - l[i][j] * c[j]
                A[b] = A[b] - c[i] * sa[i]
                B[b] = B[b] - c[i] * sb[i]
        pa, pb, pd = ra[0], rb[0], d[0][0]
        for m in range(1, 8):
            pa = jnp.where(ri == m, ra[m], pa)
            pb = jnp.where(ri == m, rb[m], pb)
            pd = jnp.where(ri == m, d[m][m], pd)
        s = 1.0 / jnp.sqrt(pd)
        upper.append(jnp.where(ci >= ri + 8 * k, pa * s, 0.0))
        lower_inv.append(jnp.where(ci <= ri + 8 * k, pb * s, 0.0))
    return jnp.concatenate(upper, axis=0), jnp.concatenate(lower_inv, axis=0)


def eliminate_by_steps(G):
    ri = lax.broadcasted_iota(jnp.int32, (W, W), 0)
    ci = lax.broadcasted_iota(jnp.int32, (W, W), 1)

    def step(j, state):
        A, B = state
        row = jnp.sum(jnp.where(ri == j, A, 0.0), axis=0, keepdims=True)
        brow = jnp.sum(jnp.where(ri == j, B, 0.0), axis=0, keepdims=True)
        col = jnp.sum(jnp.where(ci == j, A, 0.0), axis=1, keepdims=True)
        pivot = jnp.sum(jnp.where(ci[0:1] == j, row, 0.0), axis=1, keepdims=True)
        times = jnp.where(ri > j, col / pivot, 0.0)
        return A - times * row, B - times * brow

    A, B = lax.fori_loop(0, W, step, (G, (ri == ci).astype(F32)))
    s = 1.0 / jnp.sqrt(jnp.sum(jnp.where(ri == ci, A, 0.0), axis=1, keepdims=True))
    return jnp.where(ci >= ri, A * s, 0.0), jnp.where(ci <= ri, B * s, 0.0)


def dot(a, b, ca, cb):
    return lax.dot_general(a, b, (((ca,), (cb,)), ((), ())), preferred_element_type=F32)


def mm1(a, b, ca=1, cb=0):
    return dot(a.astype(BF16), b.astype(BF16), ca, cb)


def mm3(a, b, ca=1, cb=0):
    ah, al = pieces(a, 2)
    bh, bl = pieces(b, 2)
    return dot(jnp.concatenate([al, ah, ah], axis=ca), jnp.concatenate([bh, bl, bh], axis=cb), ca, cb)


def mm6(a, b, ca=1, cb=0):
    ah, am, al = pieces(a)
    bh, bm, bl = pieces(b)
    return dot(
        jnp.concatenate([al, ah, am, am, ah, ah], axis=ca), jnp.concatenate([bh, bl, bm, bh, bm, bh], axis=cb), ca, cb
    )


def factor_kernel(total, zero_ref, one_ref, inv_ref, factor_ref):
    ri = lax.broadcasted_iota(jnp.int32, (W, W), 0)
    ci = lax.broadcasted_iota(jnp.int32, (W, W), 1)
    eye = (ri == ci).astype(F32)

    def half_lower(x):
        return jnp.where(ri > ci, x, jnp.where(ri == ci, 0.5 * x, 0.0))

    hi, lo = [unpack_symmetric(zero_ref[i], one_ref[i]) * (1.0 / total) for i in range(2)]
    upper, linv = eliminate(hi)

    norm = jnp.sqrt(jnp.sum(hi * eye, axis=0, keepdims=True))
    scale, inverse = power_scale(jnp.broadcast_to(norm, (8, W)))
    wide, wide_inv = jnp.broadcast_to(scale[0:1], (W, W)), jnp.broadcast_to(inverse[0:1], (W, W))
    tall, tall_inv = wide.T, wide_inv.T
    rest = (hi * wide_inv) * tall_inv
    small = (lo * wide_inv) * tall_inv
    for t in gram_of_digits(jnp.concatenate(digits(upper * wide_inv, 8, 4), axis=1), 4, 8):
        rest, e = two_sum(rest, -t)
        small = small + e
    rest = ((rest + small) * wide) * tall

    off = mm3(mm3(linv, rest), linv, 1, 1)
    defect = eye - mm6(linv, upper, 1, 1)
    close = jnp.sum(off * off) < 1e-3

    @pl.when(close)
    def _():
        x = half_lower(off)
        for _ in range(3):
            x = half_lower(off - mm1(x, x, 1, 1))
        first_order = defect - x
        z = first_order
        for _ in range(3):
            z = first_order - mm1(x, z)
        inv_ref[...] = linv + mm3(z, linv)
        factor_ref[...] = upper + mm3(x, upper, 0, 0)

    @pl.when(jnp.logical_not(close))
    def _():
        u2, l2 = eliminate_by_steps(eye + off)
        factor = mm6(u2, upper)
        inv = mm6(l2, linv)
        inv_ref[...] = inv + mm6(eye - mm6(inv, factor, 1, 1), inv)
        factor_ref[...] = factor


def factors(zero, one, total):
    return pl.pallas_call(
        functools.partial(factor_kernel, float(total)),
        in_specs=[VM, VM],
        out_specs=[VM, VM],
        out_shape=[pltpu.VMEM((W, W), F32), jax.ShapeDtypeStruct((W, W), F32)],
        compiler_params=pltpu.CompilerParams(vmem_limit_bytes=VMEM_LIMIT),
        name="factors",
    )(on_chip(zero), on_chip(one))


def basis_kernel(s_ref, t_ref, out_ref):
    i = pl.program_id(0)
    out_ref[...] = mm6(s_ref[pl.ds(i * 8, 8)].reshape(8 * BS, W), t_ref[...], 1, 1)


def basis_of(second, inv):
    return pl.pallas_call(
        basis_kernel,
        grid=(RB // 8,),
        in_specs=[VM, VM],
        out_specs=pl.BlockSpec((8 * BS, W), lambda i: (i, 0)),
        out_shape=jax.ShapeDtypeStruct((RB * BS, W), F32),
        compiler_params=pltpu.CompilerParams(vmem_limit_bytes=VMEM_LIMIT),
        name="basis",
    )(on_chip(second), on_chip(inv))


def shards(vectors, hblocks, local_cols, ghost_lists):
    count = lax.axis_size("rows")
    me = lax.axis_index("rows")
    chips = count // 2
    core = me % 2
    odd = (me // 2) % 2

    def to_chip(i, by):
        return ((i // 2 + by) % chips) * 2 + i % 2

    pair_c = [(i, i ^ 1) for i in range(count)]
    pair_a = [(i, to_chip(i, 1 if (i // 2) % 2 == 0 else -1)) for i in range(count)]
    pair_b = [(i, to_chip(i, -1 if (i // 2) % 2 == 0 else 1)) for i in range(count)]
    pair_d = [(i, (i + (1 if i % 2 else -1)) % count) for i in range(count)]

    mine = lax.dynamic_index_in_dim(ghost_lists, me, 0, keepdims=False)
    info = jnp.stack(
        [
            1 + core,
            3 * odd,
            3 - 3 * odd,
            2 - core,
            jnp.zeros_like(me),
            jnp.where(odd == 1, AT_A, AT_B) - 16,
            jnp.where(core == 1, AT_C, AT_D) - 24,
            jnp.where(core == 1, AT_D, AT_C) - 32,
            jnp.where(odd == 1, AT_B, AT_A) - 40,
            core,
        ]
    ).astype(jnp.int32)

    v = vectors.reshape(RB, BS, W)
    move = functools.partial(lax.ppermute, axis_name="rows")

    def exchange(packs):
        return [move(x, perm=perm) for x, perm in zip(packs, (pair_c, pair_a, pair_b, pair_d))]

    v, *packs = pack(info, mine, v)
    c, a, b, d = exchange(packs)
    hs, lists, cnt = convert(hblocks, local_cols, info)
    acc = run_phase(0, GROUP, (OWN, AT_C), lists, cnt, hs, [v, c])
    first, *packs = finish_one(lists, cnt, info, mine, hs, [a, b, d], v, acc)

    c, a, b, d = exchange(packs)
    acc = run_phase(0, GROUP, (OWN, AT_C), lists, cnt, hs, [first, c])
    acc = run_phase(1, GROUP, (AT_A,), lists, cnt, hs, [a], acc)
    acc = run_phase(2, GROUP, (AT_B,), lists, cnt, hs, [b], acc)
    second, kept, sent = finish_two(lists, cnt, info, hs, d, first, v, acc)

    theirs = move(sent, perm=pair_c)
    pair = pair_add(kept[0], kept[1], theirs[0], theirs[1])
    for shift in (1, 3, 5):
        mine = jnp.stack(pair)
        one, three, two = [move(mine, perm=[(i, i ^ (by << shift)) for i in range(count)]) for by in (1, 3, 2)]
        pair = pair_add(*pair_add(*pair, one[0], one[1]), *pair_add(two[0], two[1], three[0], three[1]))
    kept = jnp.stack(pair)
    other = move(kept, perm=pair_c)
    first_core = core == 0
    zero, one = jnp.where(first_core, kept, other), jnp.where(first_core, other, kept)
    inv, factor = factors(zero, one, RB * BS * count)
    return basis_of(second, inv), factor


def solution(mesh):
    in_specs = (P("rows", None), P("rows", None, None, None), P("rows", None), P())
    out_specs = (P("rows", None), P())
    return jax.shard_map(shards, mesh=mesh, in_specs=in_specs, out_specs=out_specs, check_vma=False)
```

```python
import functools

import jax
import jax.numpy as jnp
from jax import lax
from jax.experimental import pallas as pl
from jax.experimental.pallas import tpu as pltpu
from jax.sharding import PartitionSpec as P

BS = 128
W = 128
RB = 16
GHOST = 8
NNZB = 20
NE = RB * NNZB
SPLIT = 3
BAND = W // 4
PACKED = BAND + 8
A_B_D = 4
VZERO = 48
MAXE = NE + 48
OWN, AT_C, AT_A, AT_B, AT_D = 0, 16, 24, 32, 40
LISTS = 5
GROUP = 8
FETCH, FETCHES = 10, 8
VMEM_LIMIT = 26 * 1024 * 1024
F32 = jnp.float32
BF16 = jnp.bfloat16
HIGHEST = lax.Precision.HIGHEST

ANY = pl.BlockSpec(memory_space=pl.ANY)
VM = pl.BlockSpec(memory_space=pltpu.VMEM)
SM = pl.BlockSpec(memory_space=pltpu.SMEM)


def on_chip(x):
    return pltpu.with_memory_space_constraint(x, pltpu.VMEM)


def pieces(x, count=SPLIT):
    out = []
    for _ in range(count - 1):
        part = x.astype(BF16)
        out.append(part)
        x = x - part.astype(F32)
    out.append(x.astype(BF16))
    return out


def load_table(v12_ref, v3_ref, at, block):
    hi, mid, lo = pieces(block)
    v12_ref[at, :, 0:W] = hi
    v12_ref[at, :, W : 2 * W] = mid
    v3_ref[at] = lo


def load_zero(v12_ref, v3_ref):
    v12_ref[VZERO] = jnp.zeros((BS, 2 * W), BF16)
    v3_ref[VZERO] = jnp.zeros((BS, W), BF16)


def group_of_products(which, first, count, list_ref, hs_ref, v12_ref, v3_ref, acc_ref):
    for i in range(count):
        one = list_ref[which, first + 2 * i]
        two = list_ref[which, first + 2 * i + 1]
        row = lax.shift_right_logical(one, 16)
        e1 = lax.shift_right_logical(one, 6) & 1023
        e2 = lax.shift_right_logical(two, 6) & 1023
        s1 = one & 63
        s2 = two & 63
        lhs = jnp.concatenate([hs_ref[e1], hs_ref[e2]], axis=1)
        rhs = jnp.concatenate([v12_ref[s1], v12_ref[s2]], axis=0)
        low = jnp.concatenate([v3_ref[s1], v3_ref[s2]], axis=0)
        big = jnp.dot(lhs, rhs, preferred_element_type=F32)
        small = jnp.dot(lhs[0:BS], low, preferred_element_type=F32)
        total = big[0:BS, 0:W] + (
            (big[0:BS, W:] + big[BS : 2 * BS, 0:W]) + (big[BS : 2 * BS, W:] + big[2 * BS :, 0:W] + small)
        )
        acc_ref[row] = acc_ref[row] + total


def products(which, group, list_ref, cnt_ref, *refs):
    def large(g, carry):
        group_of_products(which, g * (2 * group), group, list_ref, *refs)
        return carry

    def small(g, carry):
        group_of_products(which, begin + g * (2 * GROUP), GROUP, list_ref, *refs)
        return carry

    count = cnt_ref[which]
    begin = 0
    if group > GROUP:
        steps = lax.div(count, 2 * group)
        lax.fori_loop(0, steps, large, 0)
        begin = steps * (2 * group)
    lax.fori_loop(0, lax.div(count - begin + (2 * GROUP - 1), 2 * GROUP), small, 0)


def convert_kernel(cols_ref, info_ref, h_ref, hs_ref, list_ref, cnt_ref, buf_ref, sem_ref):
    def fetch(i, slot):
        return pltpu.make_async_copy(h_ref.at[pl.ds(i * FETCH, FETCH)], buf_ref.at[slot], sem_ref.at[slot])

    for i in range(FETCHES):
        fetch(i, i).start()
    def part(i, counts):
        slot = lax.rem(i, FETCHES)
        r = lax.div(i, NNZB // FETCH)
        counts = list(counts)
        fetch(i, slot).wait()
        for n in range(FETCH):
            e = i * FETCH + n
            hi, mid, lo = pieces(buf_ref[slot, n])
            hs_ref[e, 0:BS, :] = hi
            hs_ref[e, BS : 2 * BS, :] = mid
            hs_ref[e, 2 * BS : 3 * BS, :] = lo
            col = cols_ref[r, e - r * NNZB]
            kind = jnp.where(col < RB, 0, 1 + lax.shift_right_logical(col - RB, 3))
            v = col + info_ref[4 + kind]
            code = r * 65536 + e * 64 + v
            source = lax.shift_right_logical(v, 3)
            mine = [source < 3, source == 3, source == 4, source == 5]
            at = jnp.where(mine[0], counts[0], jnp.where(mine[1], counts[1], jnp.where(mine[2], counts[2], counts[3])))
            list_ref[jnp.maximum(source - 2, 0), at] = code
            list_ref[A_B_D, counts[4]] = code
            for p, yes in enumerate((*mine, source >= 3)):
                counts[p] = counts[p] + yes.astype(jnp.int32)

        @pl.when(i + FETCHES < NE // FETCH)
        def _():
            fetch(i + FETCHES, slot).start()

        last = ((i + 1) * FETCH == (r + 1) * NNZB).astype(jnp.int32)
        for p in range(LISTS):
            list_ref[p, counts[p]] = r * 65536 + VZERO
            counts[p] = counts[p] + (counts[p] & last)
        return tuple(counts)

    counts = lax.fori_loop(0, NE // FETCH, part, (jnp.int32(0),) * LISTS)
    for p in range(LISTS):
        cnt_ref[p] = counts[p]
        for i in range(2 * GROUP):
            list_ref[p, counts[p] + i] = VZERO


TABLE = [pltpu.VMEM((VZERO + 1, BS, 2 * W), BF16), pltpu.VMEM((VZERO + 1, BS, W), BF16)]


def convert(hblocks, local_cols, info):
    return pl.pallas_call(
        convert_kernel,
        in_specs=[SM, SM, ANY],
        out_specs=[VM, SM, SM],
        out_shape=[
            pltpu.VMEM((NE, SPLIT * BS, BS), BF16),
            jax.ShapeDtypeStruct((LISTS, MAXE), jnp.int32),
            jax.ShapeDtypeStruct((LISTS,), jnp.int32),
        ],
        scratch_shapes=[pltpu.VMEM((FETCHES, FETCH, BS, BS), F32), pltpu.SemaphoreType.DMA((FETCHES,))],
        compiler_params=pltpu.CompilerParams(vmem_limit_bytes=VMEM_LIMIT),
        cost_estimate=pl.CostEstimate(flops=NE * 4 * BS**3, bytes_accessed=NE * BS * BS * 4, transcendentals=0),
        name="convert",
    )(local_cols, info, hblocks.reshape(NE, BS, BS))


def fill_packs(info_ref, lists_ref, blocks_ref, outs):
    for t in range(4):
        for g in range(GHOST):
            outs[t][g] = blocks_ref[lists_ref[info_ref[t], g]]


PACKS = [pltpu.VMEM((GHOST, BS, W), F32)] * 4


def pack_kernel(info_ref, lists_ref, v_ref, held_ref, *rest):
    outs, sem_ref = rest[:4], rest[4]
    copies = []
    for i in range(RB // 2):
        part = pl.ds(2 * i, 2)
        copies.append(pltpu.make_async_copy(v_ref.at[part], held_ref.at[part], sem_ref.at[i]))
        copies[-1].start()
    for copy in copies:
        copy.wait()
    fill_packs(info_ref, lists_ref, held_ref, outs)


def pack(info, mine, v):
    return pl.pallas_call(
        pack_kernel,
        in_specs=[SM, SM, pl.BlockSpec(memory_space=pltpu.HBM)],
        out_specs=[VM] * 5,
        out_shape=[pltpu.VMEM((RB, BS, W), F32)] + PACKS,
        scratch_shapes=[pltpu.SemaphoreType.DMA((RB // 2,))],
        compiler_params=pltpu.CompilerParams(vmem_limit_bytes=VMEM_LIMIT),
        name="pack",
    )(info, mine, pltpu.with_memory_space_constraint(v, pltpu.HBM))


def add_list(which, group, places, bufs, list_ref, cnt_ref, hs_ref, v12_ref, v3_ref, acc_ref):
    load_zero(v12_ref, v3_ref)
    for place, buf in zip(places, bufs):
        for i in range(buf.shape[0]):
            load_table(v12_ref, v3_ref, place + i, buf[i])
    products(which, group, list_ref, cnt_ref, hs_ref, v12_ref, v3_ref, acc_ref)


def phase_kernel(which, group, places, fresh, list_ref, cnt_ref, hs_ref, *refs):
    bufs = refs[: len(places)]
    acc_ref, v12_ref, v3_ref = refs[-3:]
    if fresh:
        acc_ref[...] = jnp.zeros_like(acc_ref)
    add_list(which, group, places, bufs, list_ref, cnt_ref, hs_ref, v12_ref, v3_ref, acc_ref)


def run_phase(which, group, places, lists, cnt, hs, bufs, acc=None):
    args = [lists, cnt] + [on_chip(x) for x in (hs, *bufs)] + ([] if acc is None else [on_chip(acc)])
    return pl.pallas_call(
        functools.partial(phase_kernel, which, group, places, acc is None),
        in_specs=[SM, SM] + [VM] * (len(args) - 2),
        out_specs=VM,
        out_shape=pltpu.VMEM((RB, BS, W), F32),
        scratch_shapes=TABLE,
        input_output_aliases={} if acc is None else {len(args) - 1: 0},
        compiler_params=pltpu.CompilerParams(vmem_limit_bytes=VMEM_LIMIT),
        cost_estimate=pl.CostEstimate(
            flops=len(places) * NE * 2 * BS**3, bytes_accessed=4 * 2**20, transcendentals=0
        ),
        name=f"phase_{which}",
    )(*args)


def finish_one_kernel(
    list_ref, cnt_ref, info_ref, mine_ref, hs_ref, a_ref, b_ref, d_ref, v_ref, acc_in, first_ref, *rest
):
    outs, tables = rest[:4], rest[4:]
    for r in range(RB):
        first_ref[r] = first_ref[r] - 0.5 * v_ref[r]
    places, bufs = (AT_A, AT_B, AT_D), (a_ref, b_ref, d_ref)
    add_list(A_B_D, 2 * GROUP, places, bufs, list_ref, cnt_ref, hs_ref, *tables, first_ref)
    fill_packs(info_ref, mine_ref, first_ref, outs)


def finish_one(lists, cnt, info, mine, hs, bufs, v, acc):
    return pl.pallas_call(
        finish_one_kernel,
        in_specs=[SM] * 4 + [VM] * 6,
        out_specs=[VM] * 5,
        out_shape=[pltpu.VMEM((RB, BS, W), F32)] + PACKS,
        scratch_shapes=TABLE,
        input_output_aliases={9: 0},
        compiler_params=pltpu.CompilerParams(vmem_limit_bytes=VMEM_LIMIT),
        cost_estimate=pl.CostEstimate(flops=NE * 6 * BS**3, bytes_accessed=8 * 2**20, transcendentals=0),
        name="finish_one",
    )(lists, cnt, info, mine, on_chip(hs), *[on_chip(x) for x in bufs], on_chip(v), on_chip(acc))


def two_sum(a, b):
    s = a + b
    t = s - a
    return s, (a - (s - t)) + (b - t)


def pair_add(ah, al, bh, bl):
    s, e = two_sum(ah, bh)
    e = e + (al + bl)
    h = s + e
    return h, e - (h - s)


def power_scale(biggest):
    q = jnp.full_like(biggest, 2.0**-100)
    qi = jnp.full_like(biggest, 2.0**100)
    for e in (64, 64, 32, 16, 8, 4, 2, 1):
        t = q * (2.0**e)
        up = t <= biggest
        q = jnp.where(up, t, q)
        qi = jnp.where(up, qi * (2.0**-e), qi)
    return q * 2.0, qi * 0.5


def digits(x, bits, count):
    out = []
    x = x * (2.0 ** (bits - 1))
    for i in range(count):
        d = jnp.round(x)
        out.append(d.astype(BF16))
        x = (x - d) * (2.0**bits)
    return out


def gram_of_digits(cols, bits):
    count = len(cols)
    stacked = jnp.concatenate(cols, axis=1)
    full = lax.dot_general(stacked, stacked, (((0,), (0,)), ((), ())), preferred_element_type=F32)
    terms = []
    for w in range(2, 2 * count):
        total = None
        for i in range(1, count + 1):
            j = w - i
            if 1 <= j <= count:
                block = full[(i - 1) * W : i * W, (j - 1) * W : j * W]
                total = block if total is None else total + block
        terms.append(total * (2.0 ** (2 - bits * w)))
    return terms


def lanes_of(rows):
    return lax.broadcasted_iota(jnp.int32, (rows, W), 1)


def pack_symmetric(g):
    lane = lanes_of(BAND)
    small = lanes_of(8)

    def tail(at):
        out = jnp.zeros((8, W), F32)
        for q in range(4):
            moved = pltpu.roll(g[at + 8 * q : at + 8 * q + 8], (BAND * q - at) % W, 1)
            out = jnp.where(lax.shift_right_logical(small, 5) == q, moved, out)
        return out

    zero = jnp.where(lane < 3 * BAND, g[0:BAND], g[2 * BAND : 3 * BAND])
    one = jnp.where(lane >= BAND, g[BAND : 2 * BAND], g[3 * BAND :])
    return jnp.concatenate([zero, tail(2 * BAND)], axis=0), jnp.concatenate([one, tail(3 * BAND)], axis=0)


def unpack_symmetric(zero, one):
    lane = lanes_of(BAND)

    def tail(packed, at):
        return jnp.concatenate([pltpu.roll(packed[BAND:], (at - BAND * q) % W, 1) for q in range(4)], axis=0)

    two = jnp.where(lane >= 3 * BAND, zero[0:BAND], tail(zero, 2 * BAND))
    three = jnp.where(lane < BAND, one[0:BAND], tail(one, 3 * BAND))
    half = jnp.concatenate([zero[0:BAND], one[0:BAND], two, three], axis=0)
    i = lax.shift_right_logical(lax.broadcasted_iota(jnp.int32, (W, W), 0), 5)
    j = lax.shift_right_logical(lax.broadcasted_iota(jnp.int32, (W, W), 1), 5)
    ahead = (j - i) & 3
    return jnp.where((ahead < 2) | ((ahead == 2) & (i < 2)), half, half.T)


def finish_two_kernel(
    list_ref, cnt_ref, info_ref, hs_ref, buf_ref, first_ref, v_ref, acc_in,
    out_ref, keep_ref, send_ref, v12_ref, v3_ref,
):
    add_list(3, GROUP, (AT_D,), (buf_ref,), list_ref, cnt_ref, hs_ref, v12_ref, v3_ref, out_ref)
    biggest = jnp.zeros((BS, W), F32)
    for r in range(RB):
        second = 2.0 * (out_ref[r] - 0.5 * first_ref[r]) - v_ref[r]
        out_ref[r] = second
        biggest = jnp.maximum(biggest, jnp.abs(second))
    biggest = jnp.max(biggest, axis=0, keepdims=True)
    scale, inverse = power_scale(jnp.broadcast_to(biggest, (8, W)))
    scaled = out_ref[...].reshape(RB * BS, W) * inverse[0:1]
    terms = gram_of_digits(digits(scaled, 7, 4), 7)
    hi = terms[0]
    lo = jnp.zeros_like(hi)
    for t in terms[1:]:
        hi, e = two_sum(hi, t)
        lo = lo + e
    wide = jnp.broadcast_to(scale[0:1], (W, W))
    both = wide.T
    core = info_ref[9]
    for i, part in enumerate((hi, lo)):
        zero, one = pack_symmetric((part * wide) * both)
        keep_ref[i] = jnp.where(core == 0, zero, one)
        send_ref[i] = jnp.where(core == 0, one, zero)


def finish_two(lists, cnt, info, hs, buf, first, v, acc):
    return pl.pallas_call(
        finish_two_kernel,
        in_specs=[SM] * 3 + [VM] * 5,
        out_specs=[VM] * 3,
        out_shape=[pltpu.VMEM((RB, BS, W), F32)] + [pltpu.VMEM((2, PACKED, W), F32)] * 2,
        scratch_shapes=TABLE,
        input_output_aliases={7: 0},
        compiler_params=pltpu.CompilerParams(vmem_limit_bytes=VMEM_LIMIT),
        cost_estimate=pl.CostEstimate(flops=NE * 2 * BS**3, bytes_accessed=8 * 2**20, transcendentals=0),
        name="finish_two",
    )(lists, cnt, info, on_chip(hs), on_chip(buf), on_chip(first), on_chip(v), on_chip(acc))


def eliminate(G):
    ri = lax.broadcasted_iota(jnp.int32, (8, W), 0)
    ci = lax.broadcasted_iota(jnp.int32, (8, W), 1)
    nb = W // 8
    A = [G[8 * b : 8 * b + 8, :] for b in range(nb)]
    B = [(ci == ri + 8 * b).astype(F32) for b in range(nb)]
    upper, lower_inv = [], []
    for k in range(nb):
        lanes = [jnp.broadcast_to(A[k][:, 8 * k + c : 8 * k + c + 1], (8, W)) for c in range(8)]
        d = [[jnp.broadcast_to(lanes[c][m : m + 1, :], (8, W)) for c in range(m + 1)] for m in range(8)]
        ra = [jnp.broadcast_to(A[k][m : m + 1, :], (8, W)) for m in range(8)]
        rb = [jnp.broadcast_to(B[k][m : m + 1, :], (8, W)) for m in range(8)]
        cols = {b: [jnp.broadcast_to(A[b][:, 8 * k + c : 8 * k + c + 1], (8, W)) for c in range(8)] for b in range(k + 1, nb)}
        inv = [None] * 8
        l = [[None] * 8 for _ in range(8)]
        for i in range(8):
            inv[i] = 1.0 / d[i][i]
            for m in range(i + 1, 8):
                l[m][i] = d[m][i] * inv[i]
                for c in range(i + 1, m + 1):
                    d[m][c] = d[m][c] - l[m][i] * d[c][i]
            for m in range(i + 1, 8):
                ra[m] = ra[m] - l[m][i] * ra[i]
                rb[m] = rb[m] - l[m][i] * rb[i]
        sa = [ra[i] * inv[i] for i in range(8)]
        sb = [rb[i] * inv[i] for i in range(8)]
        for b in range(k + 1, nb):
            c = cols[b]
            for i in range(8):
                for j in range(i):
                    c[i] = c[i] - l[i][j] * c[j]
                A[b] = A[b] - c[i] * sa[i]
                B[b] = B[b] - c[i] * sb[i]
        pa, pb, pd = ra[0], rb[0], d[0][0]
        for m in range(1, 8):
            pa = jnp.where(ri == m, ra[m], pa)
            pb = jnp.where(ri == m, rb[m], pb)
            pd = jnp.where(ri == m, d[m][m], pd)
        s = 1.0 / jnp.sqrt(pd)
        upper.append(jnp.where(ci >= ri + 8 * k, pa * s, 0.0))
        lower_inv.append(jnp.where(ci <= ri + 8 * k, pb * s, 0.0))
    return jnp.concatenate(upper, axis=0), jnp.concatenate(lower_inv, axis=0)


def eliminate_by_steps(G):
    ri = lax.broadcasted_iota(jnp.int32, (W, W), 0)
    ci = lax.broadcasted_iota(jnp.int32, (W, W), 1)

    def step(j, state):
        A, B = state
        row = jnp.sum(jnp.where(ri == j, A, 0.0), axis=0, keepdims=True)
        brow = jnp.sum(jnp.where(ri == j, B, 0.0), axis=0, keepdims=True)
        col = jnp.sum(jnp.where(ci == j, A, 0.0), axis=1, keepdims=True)
        pivot = jnp.sum(jnp.where(ci[0:1] == j, row, 0.0), axis=1, keepdims=True)
        times = jnp.where(ri > j, col / pivot, 0.0)
        return A - times * row, B - times * brow

    A, B = lax.fori_loop(0, W, step, (G, (ri == ci).astype(F32)))
    s = 1.0 / jnp.sqrt(jnp.sum(jnp.where(ri == ci, A, 0.0), axis=1, keepdims=True))
    return jnp.where(ci >= ri, A * s, 0.0), jnp.where(ci <= ri, B * s, 0.0)


def dot(a, b, ca, cb):
    return lax.dot_general(a, b, (((ca,), (cb,)), ((), ())), preferred_element_type=F32)


def mm1(a, b, ca=1, cb=0):
    return dot(a.astype(BF16), b.astype(BF16), ca, cb)


def mm3(a, b, ca=1, cb=0):
    ah, al = pieces(a, 2)
    bh, bl = pieces(b, 2)
    return dot(jnp.concatenate([al, ah, ah], axis=ca), jnp.concatenate([bh, bl, bh], axis=cb), ca, cb)


def mm6(a, b, ca=1, cb=0):
    ah, am, al = pieces(a)
    bh, bm, bl = pieces(b)
    return dot(
        jnp.concatenate([al, ah, am, am, ah, ah], axis=ca), jnp.concatenate([bh, bl, bm, bh, bm, bh], axis=cb), ca, cb
    )


def factor_kernel(total, zero_ref, one_ref, inv_ref, factor_ref):
    ri = lax.broadcasted_iota(jnp.int32, (W, W), 0)
    ci = lax.broadcasted_iota(jnp.int32, (W, W), 1)
    eye = (ri == ci).astype(F32)

    def half_lower(x):
        return jnp.where(ri > ci, x, jnp.where(ri == ci, 0.5 * x, 0.0))

    hi, lo = [unpack_symmetric(zero_ref[i], one_ref[i]) * (1.0 / total) for i in range(2)]
    upper, linv = eliminate(hi)

    norm = jnp.sqrt(jnp.sum(hi * eye, axis=0, keepdims=True))
    scale, inverse = power_scale(jnp.broadcast_to(norm, (8, W)))
    wide, wide_inv = jnp.broadcast_to(scale[0:1], (W, W)), jnp.broadcast_to(inverse[0:1], (W, W))
    tall, tall_inv = wide.T, wide_inv.T
    rest = (hi * wide_inv) * tall_inv
    small = (lo * wide_inv) * tall_inv
    for t in gram_of_digits(digits(upper * wide_inv, 8, 4), 8):
        rest, e = two_sum(rest, -t)
        small = small + e
    rest = ((rest + small) * wide) * tall

    off = mm3(mm3(linv, rest), linv, 1, 1)
    defect = eye - mm6(linv, upper, 1, 1)
    close = jnp.sum(off * off) < 1e-3

    @pl.when(close)
    def _():
        x = half_lower(off)
        for _ in range(3):
            x = half_lower(off - mm1(x, x, 1, 1))
        first_order = defect - x
        z = first_order
        for _ in range(3):
            z = first_order - mm1(x, z)
        inv_ref[...] = linv + mm3(z, linv)
        factor_ref[...] = upper + mm3(x, upper, 0, 0)

    @pl.when(jnp.logical_not(close))
    def _():
        u2, l2 = eliminate_by_steps(eye + off)
        factor = mm6(u2, upper)
        inv = mm6(l2, linv)
        inv_ref[...] = inv + mm6(eye - mm6(inv, factor, 1, 1), inv)
        factor_ref[...] = factor


def factors(zero, one, total):
    return pl.pallas_call(
        functools.partial(factor_kernel, float(total)),
        in_specs=[VM, VM],
        out_specs=[VM, VM],
        out_shape=[pltpu.VMEM((W, W), F32), jax.ShapeDtypeStruct((W, W), F32)],
        compiler_params=pltpu.CompilerParams(vmem_limit_bytes=VMEM_LIMIT),
        name="factors",
    )(on_chip(zero), on_chip(one))


def basis_kernel(s_ref, t_ref, out_ref):
    i = pl.program_id(0)
    out_ref[...] = mm6(s_ref[pl.ds(i * 8, 8)].reshape(8 * BS, W), t_ref[...], 1, 1)


def basis_of(second, inv):
    return pl.pallas_call(
        basis_kernel,
        grid=(RB // 8,),
        in_specs=[VM, VM],
        out_specs=pl.BlockSpec((8 * BS, W), lambda i: (i, 0)),
        out_shape=jax.ShapeDtypeStruct((RB * BS, W), F32),
        compiler_params=pltpu.CompilerParams(vmem_limit_bytes=VMEM_LIMIT),
        name="basis",
    )(on_chip(second), on_chip(inv))


def shards(vectors, hblocks, local_cols, ghost_lists):
    count = lax.axis_size("rows")
    me = lax.axis_index("rows")
    chips = count // 2
    core = me % 2
    odd = (me // 2) % 2

    def to_chip(i, by):
        return ((i // 2 + by) % chips) * 2 + i % 2

    pair_c = [(i, i ^ 1) for i in range(count)]
    pair_a = [(i, to_chip(i, 1 if (i // 2) % 2 == 0 else -1)) for i in range(count)]
    pair_b = [(i, to_chip(i, -1 if (i // 2) % 2 == 0 else 1)) for i in range(count)]
    pair_d = [(i, (i + (1 if i % 2 else -1)) % count) for i in range(count)]

    mine = lax.dynamic_index_in_dim(ghost_lists, me, 0, keepdims=False)
    info = jnp.stack(
        [
            1 + core,
            3 * odd,
            3 - 3 * odd,
            2 - core,
            jnp.zeros_like(me),
            jnp.where(odd == 1, AT_A, AT_B) - 16,
            jnp.where(core == 1, AT_C, AT_D) - 24,
            jnp.where(core == 1, AT_D, AT_C) - 32,
            jnp.where(odd == 1, AT_B, AT_A) - 40,
            core,
        ]
    ).astype(jnp.int32)

    v = vectors.reshape(RB, BS, W)
    move = functools.partial(lax.ppermute, axis_name="rows")

    def exchange(packs):
        return [move(x, perm=perm) for x, perm in zip(packs, (pair_c, pair_a, pair_b, pair_d))]

    v, *packs = pack(info, mine, v)
    c, a, b, d = exchange(packs)
    hs, lists, cnt = convert(hblocks, local_cols, info)
    acc = run_phase(0, 2 * GROUP, (OWN, AT_C), lists, cnt, hs, [v, c])
    first, *packs = finish_one(lists, cnt, info, mine, hs, [a, b, d], v, acc)

    c, a, b, d = exchange(packs)
    acc = run_phase(0, 2 * GROUP, (OWN, AT_C), lists, cnt, hs, [first, c])
    acc = run_phase(1, GROUP, (AT_A,), lists, cnt, hs, [a], acc)
    acc = run_phase(2, GROUP, (AT_B,), lists, cnt, hs, [b], acc)
    second, kept, sent = finish_two(lists, cnt, info, hs, d, first, v, acc)

    theirs = move(sent, perm=pair_c)
    pair = pair_add(kept[0], kept[1], theirs[0], theirs[1])
    for shift in (1, 3, 5):
        mine = jnp.stack(pair)
        one, three, two = [move(mine, perm=[(i, i ^ (by << shift)) for i in range(count)]) for by in (1, 3, 2)]
        pair = pair_add(*pair_add(*pair, one[0], one[1]), *pair_add(two[0], two[1], three[0], three[1]))
    kept = jnp.stack(pair)
    other = move(kept, perm=pair_c)
    first_core = core == 0
    zero, one = jnp.where(first_core, kept, other), jnp.where(first_core, other, kept)
    inv, factor = factors(zero, one, RB * BS * count)
    return basis_of(second, inv), factor


def solution(mesh):
    in_specs = (P("rows", None), P("rows", None, None, None), P("rows", None), P())
    out_specs = (P("rows", None), P())
    return jax.shard_map(shards, mesh=mesh, in_specs=in_specs, out_specs=out_specs, check_vma=False)
```
